128 devices in a mesh: grp: 4 (over x_lo, core), brick: 32 (over x_hi, y, z).
Axes of the slice: x: 4 (x_hi: 2, x_lo: 2; x = x_hi * 2 + x_lo), y: 4, z: 4, core: 2. Of those that a mesh axis runs over, the one named last changes fastest.
Arguments:
- positions: float32 [3, 1048576], P(None, ('grp', 'brick')), may hold values from -6 to 6
- features: float32 [128, 1048576], P(None, ('grp', 'brick')), may hold values from -6 to 6
- teacher_nbr: int32 [1048576, 12], P(('grp', 'brick')), may hold values from 0 to 10239, as said below
- nbr_count: int32 [1048576], P(('grp', 'brick')), may hold values from 3 to 12
- w_rad: float32 [8, 128], replicated, may hold values from -2 to 2
- w_mix: float32 [128, 128], replicated, may hold values from -0.5 to 0.5
- w_out: float32 [128], replicated, may hold values from -0.5 to 0.5
- block_owner: int32 [32768], P(('grp', 'brick')), may hold values from 0 to 127, as said below
- block_start: int32 [32768], P(('grp', 'brick')), may hold values from 0 to 480
- atom_bead: int32 [1048576], P(('grp', 'brick')), may hold values from -1 to 31
- bead_pos: float32 [3, 65536], P(None, ('grp', 'brick')), may hold values from -6 to 6
- bead_nbr: int32 [65536, 16], P(('grp', 'brick')), may hold values from 0 to 575, as said below
- bead_weight: float32 [65536], P(('grp', 'brick')), may hold values from 0.5 to 18
- w_first: float32 [8, 128], replicated, may hold values from -2 to 2
- w_second: float32 [128], replicated, may hold values from -0.5 to 0.5
Outputs:
- atom_force: float32 [3, 1048576], P(None, ('grp', 'brick'))
- bead_force: float32 [3, 65536], P(None, ('grp', 'brick'))
- student_force: float32 [3, 65536], P(None, ('grp', 'brick'))
- grad_first: float32 [8, 128], replicated
- grad_second: float32 [128], replicated
- loss: float32 [], replicated
The draws below stay inside these ranges and needn't reach their ends.
Inputs may be any that keep to these rules, and one draw needn't show every extreme that they name: `teacher_nbr`: each slot of an atom names an atom within 1024 places of it along the chain of bricks, never itself and never past the chain's ends: a column of 1024 left ghosts, the brick's 8192 atoms and 1024 right ghosts. `block_owner`: every owner is named by exactly 2 of each brick's blocks. `bead_nbr`: each edge of a bead names a bead within 32 places of it in sequence order, never itself and never past the chain's ends: a column of 32 left ghosts, the owner's 512 beads and 32 right ghosts.
All inputs are finite; a program needn't handle non-finite values.
Results may differ from the reference program's by a relative error of at most 0.0003.
Values sent between devices are 32-bit elements; how exact they have to be, the bound alone decides.
A program may use at most 320 MiB of HBM per device.

```python
import math
import jax
import jax.numpy as jnp
from jax import lax

C = 128
NRAD = 8
H = 128
K = 12
G = 1024
ATOM_BLK = 32
BPB = 32
KB = 16
BW = 32
A_DEV = 8192
BEAD_DEV = 512
TOTAL = 1048576
BEADS = 65536


def chain_offsets(key, row_total, slot_total, per_device, reach_width):
    key_mag, key_sign = jax.random.split(key)
    magnitude = jax.random.randint(key_mag, (row_total, slot_total), 1, reach_width + 1)
    direction = jax.random.randint(key_sign, (row_total, slot_total), 0, 2) * 2 - 1
    position = jnp.arange(row_total, dtype=jnp.int32)
    local_pos = position % per_device
    slot_zero = jnp.arange(slot_total, dtype=jnp.int32)[None, :] == 0
    at_low = slot_zero & (local_pos[:, None] == 0)
    at_high = slot_zero & (local_pos[:, None] == per_device - 1)
    magnitude = jnp.where(at_low | at_high, reach_width, magnitude)
    direction = jnp.where(at_low, -1, jnp.where(at_high, 1, direction))
    offset = magnitude * direction
    target = position[:, None] + offset
    outside = (target < 0) | (target >= row_total)
    offset = jnp.where(outside, -offset, offset)
    return (local_pos[:, None] + reach_width + offset).astype(jnp.int32)


def draw_teacher_nbr(key, part):
    return chain_offsets(key, TOTAL, K, A_DEV, G)


def draw_bead_nbr(key, part):
    return chain_offsets(key, BEADS, KB, BEAD_DEV, BW)


def draw_nbr_count(key, part):
    counts = jax.random.randint(key, (TOTAL,), K // 4, K + 1)
    local_pos = jnp.arange(TOTAL, dtype=jnp.int32) % A_DEV
    counts = jnp.where(local_pos == 0, K, jnp.where(local_pos == 1, K // 4, counts))
    return counts.astype(jnp.int32)


def draw_block_owner(key, part):
    devices_all = TOTAL // A_DEV
    blocks_dev = A_DEV // ATOM_BLK
    per_owner = blocks_dev // devices_all
    key_own, key_order = jax.random.split(key)
    owner_keys = jax.random.split(key_own, devices_all)
    order_keys = jax.random.split(key_order, devices_all)
    owner_perm = jax.vmap(lambda one_key: jax.random.permutation(one_key, devices_all))(owner_keys)
    block_perm = jax.vmap(lambda one_key: jax.random.permutation(one_key, blocks_dev))(order_keys)
    chosen = jnp.take_along_axis(owner_perm, block_perm // per_owner, axis=1)
    return chosen.reshape(-1).astype(jnp.int32)


def draw_atom_bead(key, part):
    devices_all = TOTAL // A_DEV
    key_share, key_pick, key_bead = jax.random.split(key, 3)
    protein_share = jax.random.randint(key_share, (devices_all,), 3, 10)
    pick_value = jax.random.randint(key_pick, (TOTAL,), 0, 10)
    device_of = jnp.arange(TOTAL, dtype=jnp.int32) // A_DEV
    bead_rel = jax.random.randint(key_bead, (TOTAL,), 0, BPB)
    return jnp.where(pick_value < protein_share[device_of], bead_rel, -1).astype(jnp.int32)


def draw_bead_weight(key, part):
    ramp = jnp.arange(BEADS, dtype=jnp.float32) / BEADS
    noise = jnp.exp(jax.random.uniform(key, (BEADS,), jnp.float32, math.log(0.5), math.log(2.0)))
    return jnp.exp(math.log(3.0) * ramp) * noise


def plant(entries, own_key, smallest, high):
    dims = entries.shape
    index_at = [jax.random.randint(jax.random.fold_in(own_key, axis), (), 0, dims[axis]) for axis in range(len(dims))]
    entries = entries.at[tuple(index_at)].set(smallest)
    longest = dims.index(max(dims))
    index_at[longest] = (index_at[longest] + 1) % dims[longest]
    return entries.at[tuple(index_at)].set(high)


def level_of(key, dims, cuts, smallest, high):
    def one(dim, parts):
        draws = jax.random.uniform(jax.random.fold_in(jax.random.fold_in(key, 6), dim), (parts,), jnp.float32, smallest / len(cuts), high / len(cuts))
        return jnp.repeat(jnp.exp(draws), dims[dim] // parts).reshape((-1,) + (1,) * (len(dims) - dim - 1))

    factor_of = one(*cuts[0])
    for cut in cuts[1:]:
        factor_of = factor_of * one(*cut)
    return factor_of


def scatter_about(own_key, extent, scale, limit, cuts=(), held_as=jnp.bfloat16):
    result = jax.random.normal(own_key, extent, jnp.float32) * scale
    if len(cuts) > 0:
        result = level_of(own_key, extent, cuts, -0.22, 0.18) * result
    return jnp.clip(result, min=-limit, max=limit).astype(held_as)


def setup_inputs(seed: int = 0) -> dict:
    key_list = jax.random.split(jax.random.key(seed), 16)
    return {
        "positions": scatter_about(key_list[0], (3, TOTAL), 1.0, 6.0, ((1, 128),), jnp.float32),
        "features": scatter_about(key_list[1], (C, TOTAL), 1.0, 6.0, ((1, 128),), jnp.float32),
        "teacher_nbr": draw_teacher_nbr(jax.random.fold_in(key_list[15], 71), 0),
        "nbr_count": draw_nbr_count(jax.random.fold_in(key_list[15], 71), 0),
        "w_rad": scatter_about(key_list[4], (NRAD, C), NRAD ** -0.5, 2.0, (), jnp.float32),
        "w_mix": scatter_about(key_list[5], (C, C), C ** -0.5, 0.5, (), jnp.float32),
        "w_out": scatter_about(key_list[6], (C,), C ** -0.5, 0.5, (), jnp.float32),
        "block_owner": draw_block_owner(jax.random.fold_in(key_list[15], 71), 0),
        "block_start": plant(jax.random.randint(key_list[8], (TOTAL // ATOM_BLK,), 0, BEAD_DEV - BPB + 1), jax.random.fold_in(key_list[8], 1), 0, BEAD_DEV - BPB).astype(jnp.int32),
        "atom_bead": draw_atom_bead(jax.random.fold_in(key_list[15], 71), 0),
        "bead_pos": scatter_about(key_list[10], (3, BEADS), 1.0, 6.0, ((1, 128),), jnp.float32),
        "bead_nbr": draw_bead_nbr(jax.random.fold_in(key_list[15], 71), 0),
        "bead_weight": draw_bead_weight(jax.random.fold_in(key_list[15], 71), 0),
        "w_first": scatter_about(key_list[13], (NRAD, H), NRAD ** -0.5, 2.0, (), jnp.float32),
        "w_second": scatter_about(key_list[14], (H,), H ** -0.5, 0.5, (), jnp.float32),
    }


HIGHEST_PRECISION = lax.Precision.HIGHEST

def decay_rates(rate_count):
    return 0.05 * 1.6 ** jnp.arange(rate_count, dtype=jnp.float32)

def block_energy(own_pos, near_pos, own_feat, near_feat, slot_mask, w_rad, w_mix, w_out):
    offsets = near_pos - own_pos[:, None, :]
    dist_sq = lax.optimization_barrier(jnp.sum(offsets * offsets, axis=0))
    radial_basis = jnp.exp(-decay_rates(w_rad.shape[0])[:, None, None] * dist_sq[None]) * slot_mask[None]
    radial = jnp.einsum('bkn,bc->ckn', radial_basis, w_rad, precision=HIGHEST_PRECISION)
    message = lax.optimization_barrier(jnp.sum(radial * near_feat, axis=1)) / math.sqrt(near_feat.shape[1])
    mixed_feat = jnp.einsum('cn,cd->dn', message, w_mix, precision=HIGHEST_PRECISION) + own_feat
    return jnp.sum(w_out[:, None] * jax.nn.silu(mixed_feat))

def block_grads(own_pos, near_pos, own_feat, near_feat, slot_mask, w_rad, w_mix, w_out):

    def energy(first_arg, second_arg):
        return block_energy(first_arg, second_arg, own_feat, near_feat, slot_mask, w_rad, w_mix, w_out)
    energy_value, pullback = jax.vjp(energy, own_pos, near_pos)
    return pullback(jnp.ones_like(energy_value))

def student_eval(own_pos, near_pos, w_first, w_second):
    offsets = near_pos - own_pos[:, None, :]
    dist_sq = lax.optimization_barrier(jnp.sum(offsets * offsets, axis=0))
    radial_basis = jnp.exp(-decay_rates(w_first.shape[0])[:, None, None] * dist_sq[None])
    hidden = jax.nn.silu(jnp.einsum('bkn,bh->hkn', radial_basis, w_first, precision=HIGHEST_PRECISION))
    strength = jnp.einsum('hkn,h->kn', hidden, w_second, precision=HIGHEST_PRECISION)
    return lax.optimization_barrier(jnp.sum(strength[None] * offsets, axis=1))

def reference(positions, features, teacher_nbr, nbr_count, w_rad, w_mix, w_out, block_owner, block_start, atom_bead, bead_pos, bead_nbr, bead_weight, w_first, w_second):
    atom_total = positions.shape[1]
    ghost_width = G
    padded_pos = jnp.pad(positions, ((0, 0), (ghost_width, ghost_width)))
    padded_feat = jnp.pad(features, ((0, 0), (ghost_width, ghost_width)))
    device_of = (jnp.arange(atom_total, dtype=jnp.int32) // A_DEV).astype(jnp.int32)
    global_nbr = (device_of[:, None] * A_DEV + teacher_nbr).astype(jnp.int32)
    slot_mask = (jnp.arange(K, dtype=jnp.int32)[None, :] < nbr_count[:, None]).astype(jnp.float32)

    def scan_step(grad_sum, block_num):
        first_atom = (block_num * ghost_width).astype(jnp.int32)
        own_pos = lax.dynamic_slice_in_dim(padded_pos, first_atom + ghost_width, ghost_width, 1)
        own_feat = lax.dynamic_slice_in_dim(padded_feat, first_atom + ghost_width, ghost_width, 1)
        neighbours = lax.dynamic_slice_in_dim(global_nbr, first_atom, ghost_width, 0).T
        block_mask = lax.dynamic_slice_in_dim(slot_mask, first_atom, ghost_width, 0).T
        near_pos = padded_pos[:, neighbours]
        near_feat = padded_feat[:, neighbours]
        grad_own, grad_near = block_grads(own_pos, near_pos, own_feat, near_feat, block_mask, w_rad, w_mix, w_out)
        own_cols = (first_atom + ghost_width + jnp.arange(ghost_width, dtype=jnp.int32)).astype(jnp.int32)
        grad_sum = grad_sum.at[:, own_cols].add(grad_own)
        grad_sum = grad_sum.at[:, neighbours].add(grad_near)
        return (grad_sum, None)
    grad_sum, unused = lax.scan(scan_step, jnp.zeros((3, atom_total + 2 * ghost_width), jnp.float32), jnp.arange(atom_total // ghost_width, dtype=jnp.int32))
    atom_force = -grad_sum[:, ghost_width:ghost_width + atom_total]
    bead_total = bead_pos.shape[1]
    block_of = (jnp.arange(atom_total, dtype=jnp.int32) // ATOM_BLK).astype(jnp.int32)
    bead_of = block_owner[block_of] * BEAD_DEV + block_start[block_of] + atom_bead
    bead_of = jnp.where(atom_bead >= 0, bead_of, bead_total).astype(jnp.int32)
    bead_force = jax.ops.segment_sum(atom_force.T, bead_of, num_segments=bead_total + 1)[:bead_total].T
    padded_bead = jnp.pad(bead_pos, ((0, 0), (BW, BW)))
    bead_dev_of = (jnp.arange(bead_total, dtype=jnp.int32) // BEAD_DEV).astype(jnp.int32)
    global_bead_nbr = (bead_dev_of[:, None] * BEAD_DEV + bead_nbr).astype(jnp.int32)

    def bead_step(running, dev_num):
        first_bead = (dev_num * BEAD_DEV).astype(jnp.int32)
        own_pos = lax.dynamic_slice_in_dim(padded_bead, first_bead + BW, BEAD_DEV, 1)
        neighbours = lax.dynamic_slice_in_dim(global_bead_nbr, first_bead, BEAD_DEV, 0).T
        near_pos = padded_bead[:, neighbours]
        target = lax.dynamic_slice_in_dim(bead_force, first_bead, BEAD_DEV, 1)
        weights = lax.dynamic_slice_in_dim(bead_weight, first_bead, BEAD_DEV, 0)

        def block_loss(first_w, second_w):
            predicted = student_eval(own_pos, near_pos, first_w, second_w)
            residual = predicted - target
            return (jnp.sum(weights * lax.optimization_barrier(jnp.sum(residual * residual, axis=0))) / (3.0 * bead_total), predicted)
        loss_part, pullback, predicted = jax.vjp(block_loss, w_first, w_second, has_aux=True)
        grad_one, grad_two = pullback(jnp.ones_like(loss_part))
        return ((running[0] + grad_one, running[1] + grad_two, running[2] + loss_part), predicted)
    start_sums = (jnp.zeros(w_first.shape, jnp.float32), jnp.zeros(w_second.shape, jnp.float32), jnp.zeros((), jnp.float32))
    sums, predicted = lax.scan(bead_step, start_sums, jnp.arange(bead_total // BEAD_DEV, dtype=jnp.int32))
    student_force = jnp.transpose(predicted, (1, 0, 2)).reshape(3, bead_total)
    return (atom_force, bead_force, student_force, sums[0], sums[1], sums[2])
```

```python
import functools
import math

import jax
import jax.numpy as jnp
from jax import lax
from jax.experimental import pallas as pl
from jax.experimental.pallas import tpu as pltpu
from jax.sharding import PartitionSpec as P

G = 1024
BPB = 32
BW = 32
K = 12
L = 128
WIN = 24
AXES = ("grp", "brick")
F32 = jnp.float32
BF16 = jnp.bfloat16
RATES = tuple(0.05 * 1.6**b for b in range(8))


def iota(shape, dim):
    return lax.broadcasted_iota(jnp.int32, shape, dim)


def split(x):
    hi = x.astype(BF16).astype(F32)
    return hi, x - hi


def nn(a, b):
    return lax.dot_general(a, b, (((1,), (0,)), ((), ())), preferred_element_type=F32)


def nt(a, b):
    return lax.dot_general(a, b, (((1,), (1,)), ((), ())), preferred_element_type=F32)


def tn(a, b):
    return lax.dot_general(a, b, (((0,), (0,)), ((), ())), preferred_element_type=F32)


def dot3(dot, a, b):
    a_hi, a_lo = (t.astype(BF16) for t in split(a))
    b_hi, b_lo = (t.astype(BF16) for t in split(b))
    return dot(a_hi, b_hi) + dot(a_lo, b_hi) + dot(a_hi, b_lo)


def sigmoid(v):
    return 1.0 / (1.0 + jnp.exp(-v))


def rate_column():
    rows = iota((8, L), 0)
    out = jnp.zeros((8, L), F32)
    for b, rate in enumerate(RATES):
        out = jnp.where(rows == b, rate, out)
    return out


def stack_basis(basis):
    hi, lo = split(basis)
    return jnp.concatenate([hi, lo, hi, jnp.zeros_like(hi)], axis=0)


def stack_weight(weight):
    hi, lo = split(weight)
    return jnp.concatenate([hi, hi, lo, jnp.zeros_like(hi)], axis=0)


def teacher_kernel(
    idx_s, idx_v, count_v, feat, left, right, pos, w_rad, w_mix, w_out, acc, table, rows
):
    step = pl.program_id(0)

    @pl.when(step == 0)
    def _():
        acc[...] = jnp.zeros_like(acc)

        def flip(source, base):
            def one(j, carry):
                src = pl.ds(pl.multiple_of(j * L, L), L)
                dst = pl.ds(pl.multiple_of(base + j * L, L), L)
                table[dst, :] = source[:, src].T
                return carry

            lax.fori_loop(0, source.shape[1] // L, one, 0)

        flip(left, 0)
        flip(feat, G)
        flip(right, G + feat.shape[1])

    for s in range(K):
        def fetch(g, carry):
            base = pl.multiple_of(g * 64, 64)
            for j in range(64):
                r = idx_s[s, base + j]
                rows[pl.ds(s * L + base + j, 1), :] = table[pl.ds(r, 1), :]
            return carry

        lax.fori_loop(0, L // 64, fetch, 0)

    rel = idx_v[...] - step * L
    hi = rel >> 7
    lo = rel & 127
    sub = iota((L, L), 0)
    subw = iota((WIN, L), 0)
    hot = jnp.concatenate(
        [jnp.where(sub == lo[s : s + 1, :], 1.0, 0.0) for s in range(K)], axis=1
    ).astype(BF16)
    masks = [subw == hi[s : s + 1, :] for s in range(K)]
    source = jnp.concatenate([pos[j, pl.ds(step, WIN), :] for j in range(6)], axis=0)
    found = nn(source.astype(BF16), hot)
    own = [pos[c, pl.ds(step + 8, 1), :] + pos[3 + c, pl.ds(step + 8, 1), :] for c in range(3)]
    rates = rate_column()
    live = iota((K, L), 0) < count_v[0]
    offsets = []
    bases = []
    for s in range(K):
        lanes = slice(s * L, (s + 1) * L)
        d = []
        for c in range(3):
            both = found[c * WIN : (c + 1) * WIN, lanes] + found[(3 + c) * WIN : (4 + c) * WIN, lanes]
            d.append(jnp.sum(jnp.where(masks[s], both, 0.0), axis=0, keepdims=True) - own[c])
        q = d[0] * d[0] + d[1] * d[1] + d[2] * d[2]
        basis = jnp.exp(-rates * q) * jnp.where(live[s : s + 1, :], 1.0, 0.0)
        offsets.append(d)
        bases.append(stack_basis(basis))
    weight = w_rad[...]
    rate_w = rate_column() * weight
    weights = jnp.concatenate([stack_weight(weight), stack_weight(-rate_w)], axis=1)
    radial = tn(jnp.concatenate(bases, axis=1).astype(BF16), weights.astype(BF16))
    message = jnp.zeros((L, L), F32)
    for s in range(K):
        message += radial[s * L : (s + 1) * L, :L] * rows[s * L : (s + 1) * L, :]
    scale = 1.0 / math.sqrt(K)
    own_rows = table[pl.ds(pl.multiple_of(G + step * L, L), L), :]
    pre = dot3(nn, message * scale, w_mix[...]) + own_rows
    sig = sigmoid(pre)
    up = w_out[...] * (sig * (1.0 + pre * (1.0 - sig)))
    back = dot3(nt, up * scale, w_mix[...])
    ones = jnp.ones((2 * L, L), BF16)
    diag = sub == iota((L, L), 1)
    own_grad = [jnp.zeros((1, L), F32) for _ in range(3)]
    parts = [[] for _ in range(6)]
    for s in range(K):
        prod = back * rows[s * L : (s + 1) * L, :] * radial[s * L : (s + 1) * L, L:]
        prod_hi, prod_lo = split(prod)
        total = nn(jnp.concatenate([prod_hi, prod_lo], axis=1).astype(BF16), ones)
        slope = 2.0 * jnp.sum(jnp.where(diag, total, 0.0), axis=0, keepdims=True)
        for c in range(3):
            value = slope * offsets[s][c]
            own_grad[c] -= value
            v_hi, v_lo = split(value)
            parts[c].append(jnp.where(masks[s], v_hi, 0.0))
            parts[3 + c].append(jnp.where(masks[s], v_lo, 0.0))
    spread = jnp.concatenate([jnp.concatenate(p, axis=1) for p in parts], axis=0).astype(BF16)
    out = nt(spread, hot)
    for c in range(3):
        both = out[c * WIN : (c + 1) * WIN] + out[(3 + c) * WIN : (4 + c) * WIN]
        both += jnp.where(subw == 8, own_grad[c], 0.0)
        acc[c, pl.ds(step, WIN), :] += both


def teacher(idx, count, feat, left, right, ext_pos, w_rad, w_mix, w_out):
    atoms = feat.shape[1]
    steps = atoms // L
    ext_rows = (atoms + 2 * G) // L
    tall = ext_rows + 24
    pos = jnp.pad(ext_pos.reshape(3, ext_rows, L), ((0, 0), (0, 24), (0, 0)))
    hi = lax.reduce_precision(pos, 8, 7)
    pos = jnp.concatenate([hi, pos - hi], axis=0)
    whole = lambda shape: pl.BlockSpec(shape, lambda i: (0,) * len(shape))
    return pl.pallas_call(
        teacher_kernel,
        grid=(steps,),
        in_specs=[
            pl.BlockSpec((K, L), lambda i: (0, i), memory_space=pltpu.SMEM),
            pl.BlockSpec((K, L), lambda i: (0, i)),
            pl.BlockSpec((1, 1, L), lambda i: (i, 0, 0)),
            whole(feat.shape),
            whole(left.shape),
            whole(right.shape),
            whole(pos.shape),
            whole((8, L)),
            whole((L, L)),
            whole((1, L)),
        ],
        out_specs=whole((3, tall, L)),
        out_shape=jax.ShapeDtypeStruct((3, tall, L), F32),
        scratch_shapes=[
            pltpu.VMEM((atoms + 2 * G, L), F32),
            pltpu.VMEM((K * L, L), F32),
        ],
        compiler_params=pltpu.CompilerParams(vmem_limit_bytes=52 * 2**20),
        cost_estimate=pl.CostEstimate(
            flops=2 * 10**10, bytes_accessed=8 * 2**20, transcendentals=10**6
        ),
        name="teacher",
    )(
        idx,
        idx,
        count.reshape(steps, 1, L),
        feat,
        left,
        right,
        pos,
        w_rad,
        w_mix,
        w_out.reshape(1, L),
    )


KB = 16


def student_kernel(nbr, pos, w_first, w_second, force, off_out, basis_out, hid_out, slope_out):
    step = pl.program_id(0)
    rel = nbr[...] - step * L
    hi = rel >> 7
    lo = rel & 127
    lane = iota((1, L), 1)
    near = []
    own = []
    for c in range(3):
        first = pos[c, pl.ds(step, 1), :]
        second = pos[c, pl.ds(step + 1, 1), :]
        take = lambda row: jnp.take_along_axis(
            jnp.broadcast_to(row, (KB, L)), lo, axis=1, mode="promise_in_bounds"
        )
        near.append(jnp.where(hi == 0, take(first), take(second)))
        own.append(
            jnp.where(lane < L - BW, pltpu.roll(first, L - BW, 1), pltpu.roll(second, L - BW, 1))
        )
    offs = [near[c] - own[c] for c in range(3)]
    q = offs[0] * offs[0] + offs[1] * offs[1] + offs[2] * offs[2]
    rates = rate_column()
    basis = [jnp.exp(-rates * q[s : s + 1, :]) for s in range(KB)]
    stacked = jnp.concatenate([stack_basis(b) for b in basis], axis=1).astype(BF16)
    z = tn(stack_weight(w_first[...]).astype(BF16), stacked)
    w2 = w_second[...]
    out = [jnp.zeros((1, L), F32) for _ in range(3)]
    for s in range(KB):
        lanes = slice(s * L, (s + 1) * L)
        zs = z[:, lanes]
        sig = sigmoid(zs)
        hid = zs * sig
        hid_out[:, lanes] = hid
        slope_out[:, lanes] = w2 * (sig * (1.0 + zs * (1.0 - sig)))
        strength = jnp.sum(w2 * hid, axis=0, keepdims=True)
        basis_out[:, lanes] = basis[s]
        for c in range(3):
            out[c] += strength * offs[c][s : s + 1, :]
    for c in range(3):
        off_out[c] = offs[c]
        force[pl.ds(c, 1), :] = out[c]


def student(nbr, pos, w_first, w_second):
    beads = nbr.shape[1]
    steps = beads // L
    edges = KB * L
    whole = lambda shape: pl.BlockSpec(shape, lambda i: (0,) * len(shape))
    wide = lambda n: pl.BlockSpec((n, edges), lambda i: (0, i))
    return pl.pallas_call(
        student_kernel,
        grid=(steps,),
        in_specs=[
            pl.BlockSpec((KB, L), lambda i: (0, i)),
            whole(pos.shape),
            whole((8, L)),
            whole((L, 1)),
        ],
        out_specs=[
            pl.BlockSpec((3, L), lambda i: (0, i)),
            pl.BlockSpec((3, KB, L), lambda i: (0, 0, i)),
            wide(8),
            wide(L),
            wide(L),
        ],
        out_shape=[
            jax.ShapeDtypeStruct((3, beads), F32),
            jax.ShapeDtypeStruct((3, KB, beads), F32),
            jax.ShapeDtypeStruct((8, KB * beads), F32),
            jax.ShapeDtypeStruct((L, KB * beads), F32),
            jax.ShapeDtypeStruct((L, KB * beads), F32),
        ],
        compiler_params=pltpu.CompilerParams(vmem_limit_bytes=40 * 2**20),
        cost_estimate=pl.CostEstimate(
            flops=10**9, bytes_accessed=8 * 2**20, transcendentals=10**6
        ),
        name="student",
    )(nbr, pos, w_first, w_second.reshape(L, 1))


CHUNK = 1024


def mapping_kernel(force, bead, dest, start, out):
    step = pl.program_id(0)

    @pl.when(step == 0)
    def _():
        out[...] = jnp.zeros_like(out)

    b = bead[...]
    hot = iota((BPB, CHUNK), 0) == b
    highs = []
    lows = []
    for c in range(3):
        hi, lo = split(force[pl.ds(c, 1), :])
        highs.append(jnp.where(hot, hi, 0.0))
        lows.append(jnp.where(hot, lo, 0.0))
    hi, lo = split(start[...])
    first = (iota((BPB, CHUNK), 0) == 0) & (iota((BPB, CHUNK), 1) % 32 == 0)
    highs.append(jnp.where(first, hi, 0.0))
    lows.append(jnp.where(first, lo, 0.0))
    values = jnp.concatenate(highs + lows, axis=0).astype(BF16)
    place = jnp.where(iota((2 * L, CHUNK), 0) == dest[...], 1.0, 0.0).astype(BF16)
    got = nt(place, values)
    out[...] += got[:, :L] + got[:, L:]


def mapping(force, bead, dest, start):
    atoms = force.shape[1]
    row = lambda n: pl.BlockSpec((n, CHUNK), lambda i: (0, i))
    return pl.pallas_call(
        mapping_kernel,
        grid=(atoms // CHUNK,),
        in_specs=[row(3), row(1), row(1), row(1)],
        out_specs=pl.BlockSpec((2 * L, L), lambda i: (0, 0)),
        out_shape=jax.ShapeDtypeStruct((2 * L, L), F32),
        name="mapping",
    )(force, bead, dest, start)


def bead_kernel(beads_all, recv, weight, pred, offs, basis, hid, slope, force, out):
    step = pl.program_id(0)
    beads = force.shape[1]

    @pl.when(step == 0)
    def _():
        out[...] = jnp.zeros_like(out)
        turned = jnp.concatenate([recv[:L, :].T, recv[L:, :].T], axis=1)
        start = (turned[96:97, :] + 0.5).astype(jnp.int32)
        hot = jnp.where(iota((beads, 2 * L), 0) == start, 1.0, 0.0).astype(BF16)
        hi, lo = split(turned[:96, :])
        got = nt(jnp.concatenate([hi, lo], axis=0).astype(BF16), hot)
        for c in range(3):
            rows = got[c * BPB : (c + 1) * BPB] + got[96 + c * BPB : 96 + (c + 1) * BPB]
            rows = pltpu.roll(rows, 0, 1, stride=1, stride_axis=0)
            force[pl.ds(c, 1), :] = jnp.sum(rows, axis=0, keepdims=True)

    lanes = pl.ds(pl.multiple_of(step * L, L), L)
    w = weight[...]
    loss = jnp.zeros((1, L), F32)
    pull = []
    for c in range(3):
        res = pred[pl.ds(c, 1), :] - force[pl.ds(c, 1), lanes]
        loss += w * (res * res)
        pull.append((2.0 / (3.0 * beads_all)) * w * res)
    ds = sum(offs[c] * pull[c] for c in range(3))
    rows = jnp.concatenate([ds[s : s + 1, :] for s in range(KB)], axis=1)
    rows_hi, rows_lo = split(rows)
    zeros = jnp.zeros((6, rows.shape[1]), F32)
    second_in = jnp.concatenate([rows_hi, rows_lo, zeros], axis=0).astype(BF16)
    first_hi, first_lo = split(basis[...] * rows)
    first_in = jnp.concatenate([first_hi, first_lo], axis=0).astype(BF16)
    slope_hi, slope_lo = (t.astype(BF16) for t in split(slope[...]))
    hid_hi, hid_lo = (t.astype(BF16) for t in split(hid[...]))
    got_hi = nt(first_in, slope_hi)
    got_lo = nt(first_in, slope_lo)
    out[0:8, :] += got_hi[:8] + got_hi[8:] + got_lo[:8]
    two_hi = nt(second_in, hid_hi)
    two_lo = nt(second_in, hid_lo)
    out[8:9, :] += two_hi[0:1] + two_hi[1:2] + two_lo[0:1]
    out[9:10, :] += loss * (1.0 / (3.0 * beads_all))


def bead_stage(recv, weight, pred, offs, basis, hid, slope, beads_all):
    beads = pred.shape[1]
    edges = KB * L
    whole = lambda shape: pl.BlockSpec(shape, lambda i: (0,) * len(shape))
    wide = lambda n: pl.BlockSpec((n, edges), lambda i: (0, i))
    return pl.pallas_call(
        functools.partial(bead_kernel, beads_all),
        grid=(beads // L,),
        in_specs=[
            whole(recv.shape),
            pl.BlockSpec((1, L), lambda i: (0, i)),
            pl.BlockSpec((3, L), lambda i: (0, i)),
            pl.BlockSpec((3, KB, L), lambda i: (0, 0, i)),
            wide(8),
            wide(L),
            wide(L),
        ],
        out_specs=[whole((3, beads)), whole((16, L))],
        out_shape=[
            jax.ShapeDtypeStruct((3, beads), F32),
            jax.ShapeDtypeStruct((16, L), F32),
        ],
        compiler_params=pltpu.CompilerParams(vmem_limit_bytes=40 * 2**20),
        name="beads",
    )(recv, weight, pred, offs, basis, hid, slope)


def halo(cells, width):
    count = lax.axis_size(AXES)
    up = [(i, i + 1) for i in range(count - 1)]
    down = [(i + 1, i) for i in range(count - 1)]
    left = lax.ppermute(cells[:, cells.shape[1] - width :], AXES, up)
    right = lax.ppermute(cells[:, :width], AXES, down)
    return left, right


def local(
    positions,
    features,
    teacher_nbr,
    nbr_count,
    w_rad,
    w_mix,
    w_out,
    block_owner,
    block_start,
    atom_bead,
    bead_pos,
    bead_nbr,
    bead_weight,
    w_first,
    w_second,
):
    atoms = positions.shape[1]
    devices = lax.axis_size(AXES)
    count = devices
    beads = bead_pos.shape[1]
    left, right = halo(features, G)
    small = jnp.concatenate([positions[:, :G], bead_pos[:, :BW]], axis=1)
    small_end = jnp.concatenate([positions[:, atoms - G :], bead_pos[:, beads - BW :]], axis=1)
    up = [(i, i + 1) for i in range(count - 1)]
    down = [(i + 1, i) for i in range(count - 1)]
    small_left = lax.ppermute(small_end, AXES, up)
    small_right = lax.ppermute(small, AXES, down)
    ext_pos = jnp.concatenate([small_left[:, :G], positions, small_right[:, :G]], axis=1)
    bead_ext = jnp.concatenate(
        [small_left[:, G:], bead_pos, small_right[:, G:], jnp.zeros((3, L - 2 * BW), F32)], axis=1
    )
    pred, offs, basis, hid, slope = student(
        bead_nbr.T, bead_ext.reshape(3, (beads + L) // L, L), w_first, w_second
    )
    blocks = block_owner.shape[0]
    block_atoms = atoms // blocks
    order = jnp.arange(blocks, dtype=jnp.int32)
    same = (block_owner[:, None] == block_owner[None, :]) & (order[None, :] < order[:, None])
    dest = 2 * block_owner + jnp.sum(same.astype(jnp.int32), axis=1)
    spread = lambda v: jnp.broadcast_to(v[:, None], (blocks, block_atoms)).reshape(1, atoms)
    acc = teacher(
        teacher_nbr.T, nbr_count, features, left, right, ext_pos, w_rad, w_mix, w_out
    )
    ext_rows = (atoms + 2 * G) // L
    grads = acc[:, :ext_rows].reshape(3, atoms + 2 * G)
    above = lax.ppermute(grads[:, :G], AXES, down)
    below = lax.ppermute(grads[:, atoms + G :], AXES, up)
    force = -grads[:, G : atoms + G]
    force = force - jnp.pad(below, ((0, 0), (0, atoms - G))) - jnp.pad(above, ((0, 0), (atoms - G, 0)))
    outgoing = mapping(
        force, atom_bead.reshape(1, atoms), spread(dest), spread(block_start.astype(F32))
    )
    recv = lax.all_to_all(outgoing, AXES, split_axis=0, concat_axis=0, tiled=True)
    bead_force, sums = bead_stage(
        recv, bead_weight.reshape(1, beads), pred, offs, basis, hid, slope, beads * devices
    )
    sums = lax.psum(sums, AXES)
    return force, bead_force, pred, sums[:8], sums[8], jnp.sum(sums[9])


def solution(mesh):
    wide = P(None, AXES)
    tall = P(AXES, None)
    flat = P(AXES)
    return jax.shard_map(
        local,
        mesh=mesh,
        in_specs=(
            wide, wide, tall, flat, P(), P(), P(), flat, flat, flat, wide, tall, flat, P(), P(),
        ),
        out_specs=(wide, wide, wide, P(), P(), P()),
        check_vma=False,
    )
```

```python
import functools
import math

import jax
import jax.numpy as jnp
from jax import lax
from jax.experimental import pallas as pl
from jax.experimental.pallas import tpu as pltpu
from jax.sharding import PartitionSpec as P

G = 1024
BPB = 32
BW = 32
K = 12
L = 128
WIN = 24
AXES = ("grp", "brick")
F32 = jnp.float32
BF16 = jnp.bfloat16
RATES = tuple(0.05 * 1.6**b for b in range(8))


def iota(shape, dim):
    return lax.broadcasted_iota(jnp.int32, shape, dim)


def split(x):
    hi = x.astype(BF16).astype(F32)
    return hi, x - hi


def nn(a, b):
    return lax.dot_general(a, b, (((1,), (0,)), ((), ())), preferred_element_type=F32)


def nt(a, b):
    return lax.dot_general(a, b, (((1,), (1,)), ((), ())), preferred_element_type=F32)


def tn(a, b):
    return lax.dot_general(a, b, (((0,), (0,)), ((), ())), preferred_element_type=F32)


def dot3(dot, a, b):
    a_hi, a_lo = (t.astype(BF16) for t in split(a))
    b_hi, b_lo = (t.astype(BF16) for t in split(b))
    return dot(a_hi, b_hi) + dot(a_lo, b_hi) + dot(a_hi, b_lo)


def sigmoid(v):
    return 1.0 / (1.0 + jnp.exp(-v))


def rate_column():
    rows = iota((8, L), 0)
    out = jnp.zeros((8, L), F32)
    for b, rate in enumerate(RATES):
        out = jnp.where(rows == b, rate, out)
    return out


def stack_basis(basis):
    hi, lo = split(basis)
    return jnp.concatenate([hi, lo, hi, jnp.zeros_like(hi)], axis=0)


def stack_weight(weight):
    hi, lo = split(weight)
    return jnp.concatenate([hi, hi, lo, jnp.zeros_like(hi)], axis=0)


PAIR = 2 * L


def teacher_block(blk, rows, fetch, idx, count, pos, weights, w_mix, w_out, acc, table):
    rel = idx - blk * L
    hi = rel >> 7
    lo16 = (rel & 127).astype(F32).astype(BF16)
    sub16 = iota((L, L), 0).astype(F32).astype(BF16)
    subw = iota((WIN, L), 0)
    one = jnp.ones((), BF16)
    zero = jnp.zeros((), BF16)
    masks = [subw == hi[s : s + 1, :] for s in range(K)]
    source = jnp.concatenate([pos[j, pl.ds(blk, WIN), :] for j in range(6)], axis=0).astype(BF16)
    own = [pos[c, pl.ds(blk + 8, 1), :] + pos[3 + c, pl.ds(blk + 8, 1), :] for c in range(3)]
    rates = rate_column()
    live = iota((K, L), 0) < count
    hots = {}
    found = {}
    offsets = {}
    radial = {}

    def find(p):
        pieces = []
        for s in (2 * p, 2 * p + 1):
            pieces.append(jnp.where(sub16 == lo16[s : s + 1, :], one, zero))
            fetch(16)
        hots[p] = jnp.concatenate(pieces, axis=1)
        found[p] = nn(source, hots[p])
        fetch(64)

    def spread_basis(p):
        bases = []
        for j in range(2):
            s = 2 * p + j
            lanes = slice(j * L, (j + 1) * L)
            d = []
            for c in range(3):
                both = found[p][c * WIN : (c + 1) * WIN, lanes] + found[p][(3 + c) * WIN : (4 + c) * WIN, lanes]
                d.append(jnp.sum(jnp.where(masks[s], both, 0.0), axis=0, keepdims=True) - own[c])
            q = d[0] * d[0] + d[1] * d[1] + d[2] * d[2]
            basis = jnp.exp(-rates * q) * jnp.where(live[s : s + 1, :], 1.0, 0.0)
            offsets[s] = d
            bases.append(stack_basis(basis))
            fetch(16)
        radial[p] = tn(jnp.concatenate(bases, axis=1).astype(BF16), weights)
        fetch(64)

    message = [jnp.zeros((L, L), F32)]

    def add_message(p):
        fetch(0, (2 * p + 2) * L)
        for j in range(2):
            s = 2 * p + j
            message[0] += radial[p][j * L : (j + 1) * L, :L] * rows[s * L : (s + 1) * L, :]
            fetch(16)

    pairs = K // 2
    for p in range(pairs + 2):
        if p < pairs:
            find(p)
        if 0 <= p - 1 < pairs:
            spread_basis(p - 1)
        if 0 <= p - 2 < pairs:
            add_message(p - 2)
    scale = 1.0 / math.sqrt(K)
    own_rows = table[pl.ds(pl.multiple_of(G + blk * L, L), L), :]
    pre = dot3(nn, message[0] * scale, w_mix[...]) + own_rows
    fetch(32)
    sig = sigmoid(pre)
    up = w_out[...] * (sig * (1.0 + pre * (1.0 - sig)))
    fetch(32)
    back = dot3(nt, up * scale, w_mix[...])
    fetch(32)
    diag = iota((L, L), 0) == iota((L, L), 1)
    own_grad = [jnp.zeros((1, L), F32) for _ in range(3)]
    slopes = {}
    total = [None]

    def pull(p):
        for j in range(2):
            s = 2 * p + j
            prod = back * rows[s * L : (s + 1) * L, :] * radial[p][j * L : (j + 1) * L, L:]
            summed = jnp.sum(prod, axis=1, keepdims=True)
            slopes[s] = 2.0 * jnp.sum(jnp.where(diag, summed, 0.0), axis=0, keepdims=True)
            fetch(32)

    def push(p):
        parts = [[] for _ in range(6)]
        for s in (2 * p, 2 * p + 1):
            for c in range(3):
                value = slopes[s] * offsets[s][c]
                own_grad[c] -= value
                v_hi, v_lo = split(value)
                parts[c].append(jnp.where(masks[s], v_hi, 0.0))
                parts[3 + c].append(jnp.where(masks[s], v_lo, 0.0))
            fetch(16)
        spread = jnp.concatenate([jnp.concatenate(x, axis=1) for x in parts], axis=0).astype(BF16)
        got = nt(spread, hots[p])
        total[0] = got if total[0] is None else total[0] + got
        fetch(32)

    for p in range(pairs + 1):
        if p < pairs:
            pull(p)
        if p >= 1:
            push(p - 1)
    out = total[0]
    for c in range(3):
        both = out[c * WIN : (c + 1) * WIN] + out[(3 + c) * WIN : (4 + c) * WIN]
        both += jnp.where(subw == 8, own_grad[c], 0.0)
        acc[c, pl.ds(blk, WIN), :] += both
    fetch(K * L)


def fetcher(table, idx, rows):
    order = iter(range(K * L))

    done = [0]

    def fetch(n, upto=0):
        for _ in range(max(n, upto - done[0])):
            e = next(order, None)
            if e is None:
                return
            done[0] += 1
            rows[pl.ds(e, 1), :] = table[pl.ds(idx[0, e], 1), :]

    return fetch


def teacher_kernel(
    idx_h, idx_v, count_v, feat, left, right, pos, w_rad, w_mix, w_out,
    acc, table, rows_a, rows_b, idx_a, idx_b, sem_a, sem_b,
):
    blocks = idx_h.shape[0]
    acc[...] = jnp.zeros_like(acc)

    def flip(source, base):
        def one(j, carry):
            src = pl.ds(pl.multiple_of(j * L, L), L)
            dst = pl.ds(pl.multiple_of(base + j * L, L), L)
            table[dst, :] = source[:, src].T
            return carry

        lax.fori_loop(0, source.shape[1] // L, one, 0)

    def bring(blk, idx, sem):
        return pltpu.make_async_copy(idx_h.at[jnp.minimum(blk, blocks - 1)], idx, sem)

    bring(0, idx_a, sem_a).start()
    bring(1, idx_b, sem_b).start()
    flip(left, 0)
    flip(feat, G)
    flip(right, G + feat.shape[1])
    weight = w_rad[...]
    rate_w = rate_column() * weight
    weights = jnp.concatenate([stack_weight(weight), stack_weight(-rate_w)], axis=1).astype(BF16)

    def step(i, carry):
        for t, held, rows, idx, sem in ((0, rows_a, rows_a, idx_a, sem_a), (1, rows_b, rows_b, idx_b, sem_b)):
            blk = 2 * i + t
            bring(blk, idx, sem).wait()
            lanes = pl.ds(pl.multiple_of(blk * L, L), L)
            teacher_block(
                blk, held, fetcher(table, idx, rows), idx_v[:, lanes], count_v[:, lanes],
                pos, weights, w_mix, w_out, acc, table,
            )

            @pl.when(i < blocks // 2 - 1)
            def _():
                bring(blk + 2, idx, sem).start()

        return carry

    lax.fori_loop(0, blocks // 2, step, 0)


def teacher(idx, count, feat, left, right, ext_pos, w_rad, w_mix, w_out):
    atoms = feat.shape[1]
    blocks = atoms // L
    ext_rows = (atoms + 2 * G) // L
    tall = ext_rows + 24
    pos = jnp.pad(ext_pos.reshape(3, ext_rows, L), ((0, 0), (0, 24), (0, 0)))
    hi = lax.reduce_precision(pos, 8, 7)
    pos = jnp.concatenate([hi, pos - hi], axis=0)
    vmem = pl.BlockSpec(memory_space=pltpu.VMEM)
    return pl.pallas_call(
        teacher_kernel,
        in_specs=[pl.BlockSpec(memory_space=pl.ANY)] + [vmem] * 9,
        out_specs=vmem,
        out_shape=jax.ShapeDtypeStruct((3, tall, L), F32),
        scratch_shapes=[
            pltpu.VMEM((atoms + 2 * G, L), F32),
            pltpu.VMEM((K * L, L), F32),
            pltpu.VMEM((K * L, L), F32),
            pltpu.SMEM((1, K * L), jnp.int32),
            pltpu.SMEM((1, K * L), jnp.int32),
            pltpu.SemaphoreType.DMA,
            pltpu.SemaphoreType.DMA,
        ],
        compiler_params=pltpu.CompilerParams(vmem_limit_bytes=52 * 2**20),
        cost_estimate=pl.CostEstimate(
            flops=2 * 10**10, bytes_accessed=8 * 2**20, transcendentals=10**6
        ),
        name="teacher",
    )(
        idx.reshape(K, blocks, L).transpose(1, 0, 2).reshape(blocks, 1, K * L),
        idx,
        count.reshape(1, atoms),
        feat,
        left,
        right,
        pos,
        w_rad,
        w_mix,
        w_out.reshape(1, L),
    )


KB = 16


def student_kernel(nbr, pos, w_first, w_second, force, off_out, basis_out, hid_out, slope_out):
    step = pl.program_id(0)
    rel = nbr[...] - step * L
    hi = rel >> 7
    lo = rel & 127
    lane = iota((1, L), 1)
    near = []
    own = []
    for c in range(3):
        first = pos[c, pl.ds(step, 1), :]
        second = pos[c, pl.ds(step + 1, 1), :]
        take = lambda row: jnp.take_along_axis(
            jnp.broadcast_to(row, (KB, L)), lo, axis=1, mode="promise_in_bounds"
        )
        near.append(jnp.where(hi == 0, take(first), take(second)))
        own.append(
            jnp.where(lane < L - BW, pltpu.roll(first, L - BW, 1), pltpu.roll(second, L - BW, 1))
        )
    offs = [near[c] - own[c] for c in range(3)]
    q = offs[0] * offs[0] + offs[1] * offs[1] + offs[2] * offs[2]
    rates = rate_column()
    basis = [jnp.exp(-rates * q[s : s + 1, :]) for s in range(KB)]
    stacked = jnp.concatenate([stack_basis(b) for b in basis], axis=1).astype(BF16)
    z = tn(stack_weight(w_first[...]).astype(BF16), stacked)
    w2 = w_second[...]
    out = [jnp.zeros((1, L), F32) for _ in range(3)]
    for s in range(KB):
        lanes = slice(s * L, (s + 1) * L)
        zs = z[:, lanes]
        sig = sigmoid(zs)
        hid = zs * sig
        hid_out[:, lanes] = hid
        slope_out[:, lanes] = w2 * (sig * (1.0 + zs * (1.0 - sig)))
        strength = jnp.sum(w2 * hid, axis=0, keepdims=True)
        basis_out[:, lanes] = basis[s]
        for c in range(3):
            out[c] += strength * offs[c][s : s + 1, :]
    for c in range(3):
        off_out[c] = offs[c]
        force[pl.ds(c, 1), :] = out[c]


def student(nbr, pos, w_first, w_second):
    beads = nbr.shape[1]
    steps = beads // L
    edges = KB * L
    whole = lambda shape: pl.BlockSpec(shape, lambda i: (0,) * len(shape))
    wide = lambda n: pl.BlockSpec((n, edges), lambda i: (0, i))
    return pl.pallas_call(
        student_kernel,
        grid=(steps,),
        in_specs=[
            pl.BlockSpec((KB, L), lambda i: (0, i)),
            whole(pos.shape),
            whole((8, L)),
            whole((L, 1)),
        ],
        out_specs=[
            pl.BlockSpec((3, L), lambda i: (0, i)),
            pl.BlockSpec((3, KB, L), lambda i: (0, 0, i)),
            wide(8),
            wide(L),
            wide(L),
        ],
        out_shape=[
            jax.ShapeDtypeStruct((3, beads), F32),
            jax.ShapeDtypeStruct((3, KB, beads), F32),
            jax.ShapeDtypeStruct((8, KB * beads), F32),
            jax.ShapeDtypeStruct((L, KB * beads), F32),
            jax.ShapeDtypeStruct((L, KB * beads), F32),
        ],
        compiler_params=pltpu.CompilerParams(vmem_limit_bytes=40 * 2**20),
        cost_estimate=pl.CostEstimate(
            flops=10**9, bytes_accessed=8 * 2**20, transcendentals=10**6
        ),
        name="student",
    )(nbr, pos, w_first, w_second.reshape(L, 1))


CHUNK = 1024


def mapping_kernel(force, bead, dest, start, out):
    step = pl.program_id(0)

    @pl.when(step == 0)
    def _():
        out[...] = jnp.zeros_like(out)

    b = bead[...]
    hot = iota((BPB, CHUNK), 0) == b
    highs = []
    lows = []
    for c in range(3):
        hi, lo = split(force[pl.ds(c, 1), :])
        highs.append(jnp.where(hot, hi, 0.0))
        lows.append(jnp.where(hot, lo, 0.0))
    hi, lo = split(start[...])
    first = (iota((BPB, CHUNK), 0) == 0) & (iota((BPB, CHUNK), 1) % 32 == 0)
    highs.append(jnp.where(first, hi, 0.0))
    lows.append(jnp.where(first, lo, 0.0))
    values = jnp.concatenate(highs + lows, axis=0).astype(BF16)
    place = jnp.where(iota((2 * L, CHUNK), 0) == dest[...], 1.0, 0.0).astype(BF16)
    got = nt(place, values)
    out[...] += got[:, :L] + got[:, L:]


def mapping(force, bead, dest, start):
    atoms = force.shape[1]
    row = lambda n: pl.BlockSpec((n, CHUNK), lambda i: (0, i))
    return pl.pallas_call(
        mapping_kernel,
        grid=(atoms // CHUNK,),
        in_specs=[row(3), row(1), row(1), row(1)],
        out_specs=pl.BlockSpec((2 * L, L), lambda i: (0, 0)),
        out_shape=jax.ShapeDtypeStruct((2 * L, L), F32),
        name="mapping",
    )(force, bead, dest, start)


def bead_kernel(beads_all, recv, weight, pred, offs, basis, hid, slope, force, out):
    step = pl.program_id(0)
    beads = force.shape[1]

    @pl.when(step == 0)
    def _():
        out[...] = jnp.zeros_like(out)
        turned = jnp.concatenate([recv[:L, :].T, recv[L:, :].T], axis=1)
        start = (turned[96:97, :] + 0.5).astype(jnp.int32)
        hot = jnp.where(iota((beads, 2 * L), 0) == start, 1.0, 0.0).astype(BF16)
        hi, lo = split(turned[:96, :])
        got = nt(jnp.concatenate([hi, lo], axis=0).astype(BF16), hot)
        for c in range(3):
            rows = got[c * BPB : (c + 1) * BPB] + got[96 + c * BPB : 96 + (c + 1) * BPB]
            rows = pltpu.roll(rows, 0, 1, stride=1, stride_axis=0)
            force[pl.ds(c, 1), :] = jnp.sum(rows, axis=0, keepdims=True)

    lanes = pl.ds(pl.multiple_of(step * L, L), L)
    w = weight[...]
    loss = jnp.zeros((1, L), F32)
    pull = []
    for c in range(3):
        res = pred[pl.ds(c, 1), :] - force[pl.ds(c, 1), lanes]
        loss += w * (res * res)
        pull.append((2.0 / (3.0 * beads_all)) * w * res)
    ds = sum(offs[c] * pull[c] for c in range(3))
    rows = jnp.concatenate([ds[s : s + 1, :] for s in range(KB)], axis=1)
    rows_hi, rows_lo = split(rows)
    zeros = jnp.zeros((6, rows.shape[1]), F32)
    second_in = jnp.concatenate([rows_hi, rows_lo, zeros], axis=0).astype(BF16)
    first_hi, first_lo = split(basis[...] * rows)
    first_in = jnp.concatenate([first_hi, first_lo], axis=0).astype(BF16)
    slope_hi, slope_lo = (t.astype(BF16) for t in split(slope[...]))
    hid_hi, hid_lo = (t.astype(BF16) for t in split(hid[...]))
    got_hi = nt(first_in, slope_hi)
    got_lo = nt(first_in, slope_lo)
    out[0:8, :] += got_hi[:8] + got_hi[8:] + got_lo[:8]
    two_hi = nt(second_in, hid_hi)
    two_lo = nt(second_in, hid_lo)
    out[8:9, :] += two_hi[0:1] + two_hi[1:2] + two_lo[0:1]
    out[9:10, :] += loss * (1.0 / (3.0 * beads_all))


def bead_stage(recv, weight, pred, offs, basis, hid, slope, beads_all):
    beads = pred.shape[1]
    edges = KB * L
    whole = lambda shape: pl.BlockSpec(shape, lambda i: (0,) * len(shape))
    wide = lambda n: pl.BlockSpec((n, edges), lambda i: (0, i))
    return pl.pallas_call(
        functools.partial(bead_kernel, beads_all),
        grid=(beads // L,),
        in_specs=[
            whole(recv.shape),
            pl.BlockSpec((1, L), lambda i: (0, i)),
            pl.BlockSpec((3, L), lambda i: (0, i)),
            pl.BlockSpec((3, KB, L), lambda i: (0, 0, i)),
            wide(8),
            wide(L),
            wide(L),
        ],
        out_specs=[whole((3, beads)), whole((16, L))],
        out_shape=[
            jax.ShapeDtypeStruct((3, beads), F32),
            jax.ShapeDtypeStruct((16, L), F32),
        ],
        compiler_params=pltpu.CompilerParams(vmem_limit_bytes=40 * 2**20),
        name="beads",
    )(recv, weight, pred, offs, basis, hid, slope)


MESH = pl.DeviceIdType.MESH


def exchange_kernel(src, dst, held, landed, send_sem, recv_sem, own_sem):
    bricks = lax.axis_size("brick")
    total = lax.axis_size("grp") * bricks
    me = lax.axis_index("grp") * bricks + lax.axis_index("brick")
    barrier = pltpu.get_barrier_semaphore()

    def place(d):
        t = lax.rem(me + d, total)
        return t, (t // bricks, lax.rem(t, bricks))

    def greet(d, carry):
        pl.semaphore_signal(barrier, inc=1, device_id=place(d)[1], device_id_type=MESH)
        return carry

    lax.fori_loop(1, total, greet, 0)
    held[:, 0, :] = src[:total]
    held[:, 1, :] = src[total:]
    own = pltpu.make_async_copy(held.at[me], landed.at[me], own_sem)
    own.start()
    pl.semaphore_wait(barrier, total - 1)

    def send(d, carry):
        t, where = place(d)
        pltpu.make_async_remote_copy(
            src_ref=held.at[t],
            dst_ref=landed.at[me],
            send_sem=send_sem,
            recv_sem=recv_sem,
            device_id=where,
            device_id_type=MESH,
        ).start()
        return carry

    lax.fori_loop(1, total, send, 0)
    own.wait()
    most = pl.ds(0, total - 1)
    pltpu.make_async_copy(held.at[most], held.at[most], send_sem).wait()
    pltpu.make_async_copy(landed.at[most], landed.at[most], recv_sem).wait()
    dst[:total] = landed[:, 0, :]
    dst[total:] = landed[:, 1, :]


def exchange(rows):
    total = rows.shape[0] // 2
    vmem = pl.BlockSpec(memory_space=pltpu.VMEM)
    return pl.pallas_call(
        exchange_kernel,
        in_specs=[vmem],
        out_specs=vmem,
        out_shape=jax.ShapeDtypeStruct(rows.shape, F32),
        scratch_shapes=[
            pltpu.VMEM((total, 2, L), F32),
            pltpu.VMEM((total, 2, L), F32),
            pltpu.SemaphoreType.DMA,
            pltpu.SemaphoreType.DMA,
            pltpu.SemaphoreType.DMA,
        ],
        compiler_params=pltpu.CompilerParams(collective_id=1, has_side_effects=True),
        name="exchange",
    )(rows)


def reduce_kernel(x, out, first, second, third, send_sem, recv_sem):
    g = lax.axis_index("grp")
    b = lax.axis_index("brick")
    groups = first.shape[0]
    low = second.shape[0]
    high = third.shape[0]
    z = lax.rem(b, low)
    h = b // low
    stages = (
        (first, groups, g, lambda d: (lax.rem(g + d, groups), b)),
        (second, low, z, lambda d: (g, h * low + lax.rem(z + d, low))),
        (third, high, h, lambda d: (g, lax.rem(h + d, high) * low + z)),
    )
    barrier = pltpu.get_barrier_semaphore()
    partners = 0
    for _, size, _, where in stages:
        for d in range(1, size):
            pl.semaphore_signal(barrier, inc=1, device_id=where(d), device_id_type=MESH)
            partners += 1
    pl.semaphore_wait(barrier, partners)
    value = x[...]
    used = 0
    for slots, size, mine, where in stages:
        slots[pl.ds(mine, 1)] = value[None]
        copies = []
        for d in range(1, size):
            copy = pltpu.make_async_remote_copy(
                src_ref=slots.at[mine],
                dst_ref=slots.at[mine],
                send_sem=send_sem.at[used],
                recv_sem=recv_sem.at[used],
                device_id=where(d),
                device_id_type=MESH,
            )
            used += 1
            copy.start()
            copies.append(copy)
        for copy in copies:
            copy.wait()
        value = slots[0]
        for i in range(1, size):
            value = value + slots[i]
    out[...] = value


def reduce_all(x):
    groups = lax.axis_size("grp")
    bricks = lax.axis_size("brick")
    low = 4
    high = bricks // low
    count = groups + low + high - 3
    vmem = pl.BlockSpec(memory_space=pltpu.VMEM)
    return pl.pallas_call(
        reduce_kernel,
        in_specs=[vmem],
        out_specs=vmem,
        out_shape=jax.ShapeDtypeStruct(x.shape, F32),
        scratch_shapes=[pltpu.VMEM((n,) + x.shape, F32) for n in (groups, low, high)]
        + [pltpu.SemaphoreType.DMA((count,)), pltpu.SemaphoreType.DMA((count,))],
        compiler_params=pltpu.CompilerParams(collective_id=2, has_side_effects=True),
        name="reduce",
    )(x)


def halo(cells, width):
    count = lax.axis_size(AXES)
    up = [(i, i + 1) for i in range(count - 1)]
    down = [(i + 1, i) for i in range(count - 1)]
    left = lax.ppermute(cells[:, cells.shape[1] - width :], AXES, up)
    right = lax.ppermute(cells[:, :width], AXES, down)
    return left, right


def local(
    positions,
    features,
    teacher_nbr,
    nbr_count,
    w_rad,
    w_mix,
    w_out,
    block_owner,
    block_start,
    atom_bead,
    bead_pos,
    bead_nbr,
    bead_weight,
    w_first,
    w_second,
):
    atoms = positions.shape[1]
    devices = lax.axis_size(AXES)
    count = devices
    beads = bead_pos.shape[1]
    left, right = halo(features, G)
    small = jnp.concatenate([positions[:, :G], bead_pos[:, :BW]], axis=1)
    small_end = jnp.concatenate([positions[:, atoms - G :], bead_pos[:, beads - BW :]], axis=1)
    up = [(i, i + 1) for i in range(count - 1)]
    down = [(i + 1, i) for i in range(count - 1)]
    small_left = lax.ppermute(small_end, AXES, up)
    small_right = lax.ppermute(small, AXES, down)
    ext_pos = jnp.concatenate([small_left[:, :G], positions, small_right[:, :G]], axis=1)
    bead_ext = jnp.concatenate(
        [small_left[:, G:], bead_pos, small_right[:, G:], jnp.zeros((3, L - 2 * BW), F32)], axis=1
    )
    pred, offs, basis, hid, slope = student(
        bead_nbr.T, bead_ext.reshape(3, (beads + L) // L, L), w_first, w_second
    )
    blocks = block_owner.shape[0]
    block_atoms = atoms // blocks
    order = jnp.arange(blocks, dtype=jnp.int32)
    same = (block_owner[:, None] == block_owner[None, :]) & (order[None, :] < order[:, None])
    dest = block_owner + devices * jnp.sum(same.astype(jnp.int32), axis=1)
    spread = lambda v: jnp.broadcast_to(v[:, None], (blocks, block_atoms)).reshape(1, atoms)
    acc = teacher(
        teacher_nbr.T, nbr_count, features, left, right, ext_pos, w_rad, w_mix, w_out
    )
    ext_rows = (atoms + 2 * G) // L
    grads = acc[:, :ext_rows].reshape(3, atoms + 2 * G)
    above = lax.ppermute(grads[:, :G], AXES, down)
    below = lax.ppermute(grads[:, atoms + G :], AXES, up)
    force = -grads[:, G : atoms + G]
    force = force - jnp.pad(below, ((0, 0), (0, atoms - G))) - jnp.pad(above, ((0, 0), (atoms - G, 0)))
    outgoing = mapping(
        force, atom_bead.reshape(1, atoms), spread(dest), spread(block_start.astype(F32))
    )
    recv = exchange(outgoing)
    bead_force, sums = bead_stage(
        recv, bead_weight.reshape(1, beads), pred, offs, basis, hid, slope, beads * devices
    )
    sums = reduce_all(sums)
    return force, bead_force, pred, sums[:8], sums[8], jnp.sum(sums[9])


def solution(mesh):
    wide = P(None, AXES)
    tall = P(AXES, None)
    flat = P(AXES)
    return jax.shard_map(
        local,
        mesh=mesh,
        in_specs=(
            wide, wide, tall, flat, P(), P(), P(), flat, flat, flat, wide, tall, flat, P(), P(),
        ),
        out_specs=(wide, wide, wide, P(), P(), P()),
        check_vma=False,
    )
```

```python
import functools
import math

import jax
import jax.numpy as jnp
from jax import lax
from jax.experimental import pallas as pl
from jax.experimental.pallas import tpu as pltpu
from jax.sharding import PartitionSpec as P

G = 1024
BPB = 32
BW = 32
K = 12
L = 128
WIN = 24
AXES = ("grp", "brick")
F32 = jnp.float32
BF16 = jnp.bfloat16
RATES = tuple(0.05 * 1.6**b for b in range(8))


def iota(shape, dim):
    return lax.broadcasted_iota(jnp.int32, shape, dim)


def split(x):
    hi = x.astype(BF16).astype(F32)
    return hi, x - hi


def nn(a, b):
    return lax.dot_general(a, b, (((1,), (0,)), ((), ())), preferred_element_type=F32)


def nt(a, b):
    return lax.dot_general(a, b, (((1,), (1,)), ((), ())), preferred_element_type=F32)


def tn(a, b):
    return lax.dot_general(a, b, (((0,), (0,)), ((), ())), preferred_element_type=F32)


def dot3(dot, a, b):
    a_hi, a_lo = (t.astype(BF16) for t in split(a))
    b_hi, b_lo = (t.astype(BF16) for t in split(b))
    return dot(a_hi, b_hi) + dot(a_lo, b_hi) + dot(a_hi, b_lo)


def sigmoid(v):
    return 1.0 / (1.0 + jnp.exp(-v))


def rate_column():
    rows = iota((8, L), 0)
    out = jnp.zeros((8, L), F32)
    for b, rate in enumerate(RATES):
        out = jnp.where(rows == b, rate, out)
    return out


def stack_basis(basis):
    hi, lo = split(basis)
    return jnp.concatenate([hi, lo, hi, jnp.zeros_like(hi)], axis=0)


def stack_weight(weight):
    hi, lo = split(weight)
    return jnp.concatenate([hi, hi, lo, jnp.zeros_like(hi)], axis=0)


PAIR = 2 * L


def forward_part(blk, held, idx_s, idx, count, pos, weights, table):
    rows, slope_w, hots, offs, sent = held
    rel = idx - blk * L
    hi = rel >> 7
    lo16 = (rel & 127).astype(F32).astype(BF16)
    sub16 = iota((L, L), 0).astype(F32).astype(BF16)
    subw = iota((WIN, L), 0)
    one = jnp.ones((), BF16)
    zero = jnp.zeros((), BF16)
    source = jnp.concatenate([pos[j, pl.ds(blk, WIN), :] for j in range(6)], axis=0).astype(BF16)
    own = [pos[c, pl.ds(blk + 8, 1), :] + pos[3 + c, pl.ds(blk + 8, 1), :] for c in range(3)]
    rates = rate_column()
    live = iota((K, L), 0) < count
    found = {}
    radial = {}
    order = iter(range(K * L))
    done = [0]

    def fetch(n, upto=0):
        for _ in range(max(n, upto - done[0])):
            e = next(order, None)
            if e is None:
                return
            done[0] += 1
            rows[pl.ds(e, 1), :] = table[pl.ds(idx_s[0, e], 1), :]

    message = jnp.zeros((L, L), F32)
    pairs = K // 2
    for p in range(pairs + 2):
        if p < pairs:
            pieces = []
            for s in (2 * p, 2 * p + 1):
                pieces.append(jnp.where(sub16 == lo16[s : s + 1, :], one, zero))
                fetch(FETCH)
            hot = jnp.concatenate(pieces, axis=1)
            hots[:, p * PAIR : (p + 1) * PAIR] = hot
            found[p] = nn(source, hot)
            fetch(FETCH)
            yield
        if 0 <= p - 1 < pairs:
            r = p - 1
            bases = []
            for j in range(2):
                s = 2 * r + j
                lanes = slice(j * L, (j + 1) * L)
                mask = subw == hi[s : s + 1, :]
                d = []
                for c in range(3):
                    both = found[r][c * WIN : (c + 1) * WIN, lanes] + found[r][(3 + c) * WIN : (4 + c) * WIN, lanes]
                    d.append(jnp.sum(jnp.where(mask, both, 0.0), axis=0, keepdims=True) - own[c])
                    offs[pl.ds(c * 16 + s, 1), :] = d[c]
                q = d[0] * d[0] + d[1] * d[1] + d[2] * d[2]
                basis = jnp.exp(-rates * q) * jnp.where(live[s : s + 1, :], 1.0, 0.0)
                bases.append(stack_basis(basis))
                fetch(FETCH)
                yield
            both = tn(jnp.concatenate(bases, axis=1).astype(BF16), weights)
            radial[r] = both[:, :L]
            slope_w[r * PAIR : (r + 1) * PAIR, :] = both[:, L:]
            fetch(FETCH)
            yield
        if 0 <= p - 2 < pairs:
            r = p - 2
            fetch(0, (2 * r + 2) * L)
            for j in range(2):
                s = 2 * r + j
                message += radial[r][j * L : (j + 1) * L] * rows[s * L : (s + 1) * L, :]
            yield
    sent[...] = message


def backward_part(blk, held, idx, mix, w_out, acc, table):
    rows, slope_w, hots, offs, sent = held
    hi = (idx - blk * L) >> 7
    subw = iota((WIN, L), 0)
    mix_hh, mix_l, turn_hh, turn_l = mix
    scale = 1.0 / math.sqrt(K)

    def product(x, w_hh, w_l):
        x_hi, x_lo = split(x)
        wide = jnp.concatenate([x_hi, x_lo], axis=1).astype(BF16)
        return nn(wide, w_hh) + nn(wide[:, :L], w_l)

    own_rows = table[pl.ds(pl.multiple_of(G + blk * L, L), L), :]
    mixed = product(sent[...] * scale, mix_hh, mix_l)
    yield
    pre = mixed + own_rows
    sig = sigmoid(pre)
    up = w_out[...] * (sig * (1.0 + pre * (1.0 - sig)))
    yield
    back = product(up * scale, turn_hh, turn_l)
    yield
    diag = iota((L, L), 0) == iota((L, L), 1)
    own_grad = [jnp.zeros((1, L), F32) for _ in range(3)]
    slopes = {}
    out = None
    pairs = K // 2
    for p in range(pairs + 1):
        if p < pairs:
            for j in range(2):
                s = 2 * p + j
                prod = back * rows[s * L : (s + 1) * L, :] * slope_w[s * L : (s + 1) * L, :]
                summed = jnp.sum(prod, axis=1, keepdims=True)
                slopes[s] = 2.0 * jnp.sum(jnp.where(diag, summed, 0.0), axis=0, keepdims=True)
                yield
        if p >= 1:
            r = p - 1
            parts = [[] for _ in range(6)]
            for s in (2 * r, 2 * r + 1):
                mask = subw == hi[s : s + 1, :]
                for c in range(3):
                    value = slopes[s] * offs[pl.ds(c * 16 + s, 1), :]
                    own_grad[c] -= value
                    v_hi, v_lo = split(value)
                    parts[c].append(jnp.where(mask, v_hi, 0.0))
                    parts[3 + c].append(jnp.where(mask, v_lo, 0.0))
            spread = jnp.concatenate([jnp.concatenate(x, axis=1) for x in parts], axis=0).astype(BF16)
            yield
            got = nt(spread, hots[:, r * PAIR : (r + 1) * PAIR])
            out = got if out is None else out + got
            yield
    for c in range(3):
        both = out[c * WIN : (c + 1) * WIN] + out[(3 + c) * WIN : (4 + c) * WIN]
        both += jnp.where(subw == 8, own_grad[c], 0.0)
        acc[c, pl.ds(blk, WIN), :] += both


FETCH = 40


def run_beside(one, two):
    alive = [one, two]
    while alive:
        for part in list(alive):
            if next(part, 1) == 1:
                alive.remove(part)


def teacher_kernel(
    idx_h, idx_v, count_v, feat, left, right, pos, w_rad, w_mix, w_out,
    acc, table, idx_a, idx_b, sem_a, sem_b, *held,
):
    blocks = idx_h.shape[0]
    acc[...] = jnp.zeros_like(acc)
    held_a, held_b = held[:5], held[5:]

    def flip(source, base):
        def one(j, carry):
            src = pl.ds(pl.multiple_of(j * L, L), L)
            dst = pl.ds(pl.multiple_of(base + j * L, L), L)
            table[dst, :] = source[:L, src].T
            return carry

        lax.fori_loop(0, source.shape[1] // L, one, 0)

    def bring(blk, idx, sem):
        return pltpu.make_async_copy(idx_h.at[jnp.minimum(blk, blocks - 1)], idx, sem)

    bring(0, idx_a, sem_a).start()
    bring(1, idx_b, sem_b).start()
    flip(left, 0)
    flip(feat, G)
    flip(right, G + feat.shape[1])
    weight = w_rad[...]
    rate_w = rate_column() * weight
    weights = jnp.concatenate([stack_weight(weight), stack_weight(-rate_w)], axis=1).astype(BF16)
    mix = []
    for w in (w_mix[...], w_mix[...].T):
        w_hi, w_lo = split(w)
        mix += [jnp.concatenate([w_hi, w_hi], axis=0).astype(BF16), w_lo.astype(BF16)]

    def forward(blk, held, idx_s):
        lanes = pl.ds(pl.multiple_of(blk * L, L), L)
        return forward_part(blk, held, idx_s, idx_v[:, lanes], count_v[:, lanes], pos, weights, table)

    def backward(blk, held):
        lanes = pl.ds(pl.multiple_of(blk * L, L), L)
        return backward_part(blk, held, idx_v[:, lanes], mix, w_out, acc, table)

    bring(0, idx_a, sem_a).wait()
    for _ in forward(0, held_a, idx_a):
        pass
    bring(2, idx_a, sem_a).start()

    def step(i, carry):
        for t, old, new, idx, sem in ((0, held_a, held_b, idx_b, sem_b), (1, held_b, held_a, idx_a, sem_a)):
            blk = 2 * i + t
            bring(blk + 1, idx, sem).wait()
            run_beside(backward(blk, old), forward(jnp.minimum(blk + 1, blocks - 1), new, idx))

            @pl.when(i < blocks // 2 - 1)
            def _():
                bring(blk + 3, idx, sem).start()

        return carry

    lax.fori_loop(0, blocks // 2, step, 0)


def teacher(idx, count, feat, left, right, ext_pos, w_rad, w_mix, w_out):
    atoms = feat.shape[1]
    blocks = atoms // L
    ext_rows = (atoms + 2 * G) // L
    tall = ext_rows + 24
    pos = jnp.pad(ext_pos.reshape(3, ext_rows, L), ((0, 0), (0, 24), (0, 0)))
    hi = lax.reduce_precision(pos, 8, 7)
    pos = jnp.concatenate([hi, pos - hi], axis=0)
    vmem = pl.BlockSpec(memory_space=pltpu.VMEM)
    return pl.pallas_call(
        teacher_kernel,
        in_specs=[pl.BlockSpec(memory_space=pl.ANY)] + [vmem] * 9,
        out_specs=vmem,
        out_shape=jax.ShapeDtypeStruct((3, tall, L), F32),
        scratch_shapes=[
            pltpu.VMEM((atoms + 2 * G, L), F32),
            pltpu.SMEM((1, K * L), jnp.int32),
            pltpu.SMEM((1, K * L), jnp.int32),
            pltpu.SemaphoreType.DMA,
            pltpu.SemaphoreType.DMA,
        ]
        + 2
        * [
            pltpu.VMEM((K * L, L), F32),
            pltpu.VMEM((K * L, L), F32),
            pltpu.VMEM((L, K * L), BF16),
            pltpu.VMEM((48, L), F32),
            pltpu.VMEM((L, L), F32),
        ],
        compiler_params=pltpu.CompilerParams(vmem_limit_bytes=52 * 2**20),
        cost_estimate=pl.CostEstimate(
            flops=2 * 10**10, bytes_accessed=8 * 2**20, transcendentals=10**6
        ),
        name="teacher",
    )(
        idx.reshape(K, blocks, L).transpose(1, 0, 2).reshape(blocks, 1, K * L),
        idx,
        count.reshape(1, atoms),
        feat,
        left,
        right,
        pos,
        w_rad,
        w_mix,
        w_out.reshape(1, L),
    )


KB = 16


def student_terms(offs, w_first, w2):
    q = offs[0] * offs[0] + offs[1] * offs[1] + offs[2] * offs[2]
    rates = rate_column()
    basis = [jnp.exp(-rates * q[s : s + 1, :]) for s in range(KB)]
    stacked = jnp.concatenate([stack_basis(b) for b in basis], axis=1).astype(BF16)
    z = tn(stack_weight(w_first).astype(BF16), stacked)
    return basis, z


def student_kernel(nbr, pos, w_first, w_second, force, off_out):
    step = pl.program_id(0)
    rel = nbr[...] - step * L
    hi = rel >> 7
    lo = rel & 127
    lane = iota((1, L), 1)
    near = []
    own = []
    for c in range(3):
        first = pos[c, pl.ds(step, 1), :]
        second = pos[c, pl.ds(step + 1, 1), :]
        take = lambda row: jnp.take_along_axis(
            jnp.broadcast_to(row, (KB, L)), lo, axis=1, mode="promise_in_bounds"
        )
        near.append(jnp.where(hi == 0, take(first), take(second)))
        own.append(
            jnp.where(lane < L - BW, pltpu.roll(first, L - BW, 1), pltpu.roll(second, L - BW, 1))
        )
    offs = [near[c] - own[c] for c in range(3)]
    w2 = w_second[...]
    basis, z = student_terms(offs, w_first[...], w2)
    out = [jnp.zeros((1, L), F32) for _ in range(3)]
    for s in range(KB):
        zs = z[:, s * L : (s + 1) * L]
        strength = jnp.sum(w2 * (zs * sigmoid(zs)), axis=0, keepdims=True)
        for c in range(3):
            out[c] += strength * offs[c][s : s + 1, :]
    for c in range(3):
        off_out[c] = offs[c]
        force[pl.ds(c, 1), :] = out[c]


def student(nbr, pos, w_first, w_second):
    beads = nbr.shape[1]
    whole = lambda shape: pl.BlockSpec(shape, lambda i: (0,) * len(shape))
    return pl.pallas_call(
        student_kernel,
        grid=(beads // L,),
        in_specs=[
            pl.BlockSpec((KB, L), lambda i: (0, i)),
            whole(pos.shape),
            whole((8, L)),
            whole((L, 1)),
        ],
        out_specs=[
            pl.BlockSpec((3, L), lambda i: (0, i)),
            pl.BlockSpec((3, KB, L), lambda i: (0, 0, i)),
        ],
        out_shape=[
            jax.ShapeDtypeStruct((3, beads), F32),
            jax.ShapeDtypeStruct((3, KB, beads), F32),
        ],
        compiler_params=pltpu.CompilerParams(vmem_limit_bytes=40 * 2**20),
        cost_estimate=pl.CostEstimate(
            flops=10**9, bytes_accessed=10**6, transcendentals=10**6
        ),
        name="student",
    )(nbr, pos, w_first, w_second)


CHUNK = 1024


def mapping_kernel(force, bead, dest, start, out):
    step = pl.program_id(0)

    @pl.when(step == 0)
    def _():
        out[...] = jnp.zeros_like(out)

    b = bead[...]
    hot = iota((BPB, CHUNK), 0) == b
    highs = []
    lows = []
    for c in range(3):
        hi, lo = split(force[pl.ds(c, 1), :])
        highs.append(jnp.where(hot, hi, 0.0))
        lows.append(jnp.where(hot, lo, 0.0))
    hi, lo = split(start[...])
    first = (iota((BPB, CHUNK), 0) == 0) & (iota((BPB, CHUNK), 1) % 32 == 0)
    highs.append(jnp.where(first, hi, 0.0))
    lows.append(jnp.where(first, lo, 0.0))
    values = jnp.concatenate(highs + lows, axis=0).astype(BF16)
    place = jnp.where(iota((2 * L, CHUNK), 0) == dest[...], 1.0, 0.0).astype(BF16)
    got = nt(place, values)
    out[...] += got[:, :L] + got[:, L:]


def mapping(force, bead, dest, start):
    atoms = force.shape[1]
    row = lambda n: pl.BlockSpec((n, CHUNK), lambda i: (0, i))
    return pl.pallas_call(
        mapping_kernel,
        grid=(atoms // CHUNK,),
        in_specs=[row(3), row(1), row(1), row(1)],
        out_specs=pl.BlockSpec((2 * L, L), lambda i: (0, 0)),
        out_shape=jax.ShapeDtypeStruct((2 * L, L), F32),
        name="mapping",
    )(force, bead, dest, start)


def bead_kernel(beads_all, recv, weight, pred, offs, w_first, w_second, force, out):
    step = pl.program_id(0)
    beads = force.shape[1]

    @pl.when(step == 0)
    def _():
        out[...] = jnp.zeros_like(out)
        turned = jnp.concatenate([recv[:L, :].T, recv[L:, :].T], axis=1)
        start = (turned[96:97, :] + 0.5).astype(jnp.int32)
        hot = jnp.where(iota((beads, 2 * L), 0) == start, 1.0, 0.0).astype(BF16)
        hi, lo = split(turned[:96, :])
        got = nt(jnp.concatenate([hi, lo], axis=0).astype(BF16), hot)
        for c in range(3):
            rows = got[c * BPB : (c + 1) * BPB] + got[96 + c * BPB : 96 + (c + 1) * BPB]
            rows = pltpu.roll(rows, 0, 1, stride=1, stride_axis=0)
            force[pl.ds(c, 1), :] = jnp.sum(rows, axis=0, keepdims=True)

    lanes = pl.ds(pl.multiple_of(step * L, L), L)
    w = weight[...]
    loss = jnp.zeros((1, L), F32)
    pull = []
    for c in range(3):
        res = pred[pl.ds(c, 1), :] - force[pl.ds(c, 1), lanes]
        loss += w * (res * res)
        pull.append((2.0 / (3.0 * beads_all)) * w * res)
    ds = sum(offs[c] * pull[c] for c in range(3))
    rows = jnp.concatenate([ds[s : s + 1, :] for s in range(KB)], axis=1)
    rows_hi, rows_lo = split(rows)
    zeros = jnp.zeros((6, rows.shape[1]), F32)
    second_in = jnp.concatenate([rows_hi, rows_lo, zeros], axis=0).astype(BF16)
    w2 = w_second[...]
    basis, z = student_terms([offs[c] for c in range(3)], w_first[...], w2)
    sig = sigmoid(z)
    slope = w2 * (sig * (1.0 + z * (1.0 - sig)))
    first_hi, first_lo = split(jnp.concatenate(basis, axis=1) * rows)
    first_in = jnp.concatenate([first_hi, first_lo], axis=0).astype(BF16)
    slope_hi, slope_lo = (t.astype(BF16) for t in split(slope))
    hid_hi, hid_lo = (t.astype(BF16) for t in split(z * sig))
    got_hi = nt(first_in, slope_hi)
    got_lo = nt(first_in, slope_lo)
    out[0:8, :] += got_hi[:8] + got_hi[8:] + got_lo[:8]
    two_hi = nt(second_in, hid_hi)
    two_lo = nt(second_in, hid_lo)
    out[8:9, :] += two_hi[0:1] + two_hi[1:2] + two_lo[0:1]
    out[9:10, :] += loss * (1.0 / (3.0 * beads_all))


def bead_stage(recv, weight, pred, offs, w_first, w_second, beads_all):
    beads = pred.shape[1]
    whole = lambda shape: pl.BlockSpec(shape, lambda i: (0,) * len(shape))
    return pl.pallas_call(
        functools.partial(bead_kernel, beads_all),
        grid=(beads // L,),
        in_specs=[
            whole(recv.shape),
            pl.BlockSpec((1, L), lambda i: (0, i)),
            pl.BlockSpec((3, L), lambda i: (0, i)),
            pl.BlockSpec((3, KB, L), lambda i: (0, 0, i)),
            whole((8, L)),
            whole((L, 1)),
        ],
        out_specs=[whole((3, beads)), whole((16, L))],
        out_shape=[
            jax.ShapeDtypeStruct((3, beads), F32),
            jax.ShapeDtypeStruct((16, L), F32),
        ],
        compiler_params=pltpu.CompilerParams(vmem_limit_bytes=40 * 2**20),
        name="beads",
    )(recv, weight, pred, offs, w_first, w_second)


MESH = pl.DeviceIdType.MESH


LOW = 4


def exchange_kernel(src, dst, first, packed, second, send_sem, recv_sem):
    g = lax.axis_index("grp")
    b = lax.axis_index("brick")
    near = lax.axis_size("grp") * LOW
    far = lax.axis_size("brick") // LOW
    h = b // LOW
    z = lax.rem(b, LOW)
    mine = g * LOW + z
    span = 2 * far

    def near_place(d):
        j = lax.rem(mine + d, near)
        return j, (j // LOW, h * LOW + lax.rem(j, LOW))

    def far_place(d):
        j = lax.rem(h + d, far)
        return j, (g, j * LOW + z)

    barrier = pltpu.get_barrier_semaphore()
    for count, place in ((near, near_place), (far, far_place)):
        for d in range(1, count):
            pl.semaphore_signal(barrier, inc=1, device_id=place(d)[1], device_id_type=MESH)
    pl.semaphore_wait(barrier, near + far - 2)
    at_mine = pl.ds(pl.multiple_of(mine * span, span), span)
    copies = []
    for d in range(1, near):
        j, where = near_place(d)
        copies.append(
            pltpu.make_async_remote_copy(
                src_ref=src.at[pl.ds(pl.multiple_of(j * span, span), span)],
                dst_ref=first.at[at_mine],
                send_sem=send_sem.at[d - 1],
                recv_sem=recv_sem.at[d - 1],
                device_id=where,
                device_id_type=MESH,
            )
        )
        copies[-1].start()
    first[at_mine, :] = src[at_mine, :]
    for copy in copies:
        copy.wait()
    for j in range(far):
        packed[j] = first[pl.ds(j, 2 * near, stride=far), :]
    copies = []
    for d in range(1, far):
        j, where = far_place(d)
        copies.append(
            pltpu.make_async_remote_copy(
                src_ref=packed.at[j],
                dst_ref=second.at[h],
                send_sem=send_sem.at[near + d - 2],
                recv_sem=recv_sem.at[near + d - 2],
                device_id=where,
                device_id_type=MESH,
            )
        )
        copies[-1].start()
    second[pl.ds(h, 1)] = packed[pl.ds(h, 1)]
    for copy in copies:
        copy.wait()
    for j in range(far):
        dst[j * 2 * near : (j + 1) * 2 * near, :] = second[j]


def exchange(rows):
    near = lax.axis_size("grp") * LOW
    far = lax.axis_size("brick") // LOW
    vmem = pl.BlockSpec(memory_space=pltpu.VMEM)
    return pl.pallas_call(
        exchange_kernel,
        in_specs=[vmem],
        out_specs=vmem,
        out_shape=jax.ShapeDtypeStruct(rows.shape, F32),
        scratch_shapes=[
            pltpu.VMEM(rows.shape, F32),
            pltpu.VMEM((far, 2 * near, L), F32),
            pltpu.VMEM((far, 2 * near, L), F32),
            pltpu.SemaphoreType.DMA((near + far - 2,)),
            pltpu.SemaphoreType.DMA((near + far - 2,)),
        ],
        compiler_params=pltpu.CompilerParams(collective_id=1, has_side_effects=True),
        name="exchange",
    )(rows)


def reduce_kernel(x, out, first, second, third, send_sem, recv_sem):
    g = lax.axis_index("grp")
    b = lax.axis_index("brick")
    groups = first.shape[0]
    low = second.shape[0]
    high = third.shape[0]
    z = lax.rem(b, low)
    h = b // low
    stages = (
        (first, groups, g, lambda d: (lax.rem(g + d, groups), b)),
        (second, low, z, lambda d: (g, h * low + lax.rem(z + d, low))),
        (third, high, h, lambda d: (g, lax.rem(h + d, high) * low + z)),
    )
    barrier = pltpu.get_barrier_semaphore()
    partners = 0
    for _, size, _, where in stages:
        for d in range(1, size):
            pl.semaphore_signal(barrier, inc=1, device_id=where(d), device_id_type=MESH)
            partners += 1
    pl.semaphore_wait(barrier, partners)
    value = x[...]
    used = 0
    for slots, size, mine, where in stages:
        slots[pl.ds(mine, 1)] = value[None]
        copies = []
        for d in range(1, size):
            copy = pltpu.make_async_remote_copy(
                src_ref=slots.at[mine],
                dst_ref=slots.at[mine],
                send_sem=send_sem.at[used],
                recv_sem=recv_sem.at[used],
                device_id=where(d),
                device_id_type=MESH,
            )
            used += 1
            copy.start()
            copies.append(copy)
        for copy in copies:
            copy.wait()
        value = slots[0]
        for i in range(1, size):
            value = value + slots[i]
    out[...] = value


def reduce_all(x):
    groups = lax.axis_size("grp")
    bricks = lax.axis_size("brick")
    low = LOW
    high = bricks // low
    count = groups + low + high - 3
    vmem = pl.BlockSpec(memory_space=pltpu.VMEM)
    return pl.pallas_call(
        reduce_kernel,
        in_specs=[vmem],
        out_specs=vmem,
        out_shape=jax.ShapeDtypeStruct(x.shape, F32),
        scratch_shapes=[pltpu.VMEM((n,) + x.shape, F32) for n in (groups, low, high)]
        + [pltpu.SemaphoreType.DMA((count,)), pltpu.SemaphoreType.DMA((count,))],
        compiler_params=pltpu.CompilerParams(collective_id=2, has_side_effects=True),
        name="reduce",
    )(x)


def local(
    positions,
    features,
    teacher_nbr,
    nbr_count,
    w_rad,
    w_mix,
    w_out,
    block_owner,
    block_start,
    atom_bead,
    bead_pos,
    bead_nbr,
    bead_weight,
    w_first,
    w_second,
):
    atoms = positions.shape[1]
    devices = lax.axis_size(AXES)
    count = devices
    beads = bead_pos.shape[1]
    up = [(i, i + 1) for i in range(count - 1)]
    down = [(i + 1, i) for i in range(count - 1)]

    def payload(feat, pos, bead):
        tail = jnp.concatenate([pos, jnp.pad(bead, ((0, 2), (0, G - BW)))], axis=0)
        return jnp.concatenate([feat, tail], axis=0)

    left = lax.ppermute(
        payload(features[:, atoms - G :], positions[:, atoms - G :], bead_pos[:, beads - BW :]), AXES, up
    )
    right = lax.ppermute(payload(features[:, :G], positions[:, :G], bead_pos[:, :BW]), AXES, down)
    ext_pos = jnp.concatenate([left[L : L + 3], positions, right[L : L + 3]], axis=1)
    bead_ext = jnp.concatenate(
        [left[L + 3 : L + 6, :BW], bead_pos, right[L + 3 : L + 6, :BW], jnp.zeros((3, L - 2 * BW), F32)],
        axis=1,
    )
    second = w_second.reshape(L, 1)
    pred, offs = student(bead_nbr.T, bead_ext.reshape(3, (beads + L) // L, L), w_first, second)
    blocks = block_owner.shape[0]
    block_atoms = atoms // blocks
    order = jnp.arange(blocks, dtype=jnp.int32)
    same = (block_owner[:, None] == block_owner[None, :]) & (order[None, :] < order[:, None])
    rank = jnp.sum(same.astype(jnp.int32), axis=1)
    bricks = lax.axis_size("brick")
    far = bricks // LOW
    near_at = (block_owner // bricks) * LOW + block_owner % LOW
    dest = near_at * 2 * far + rank * far + (block_owner % bricks) // LOW
    spread = lambda v: jnp.broadcast_to(v[:, None], (blocks, block_atoms)).reshape(1, atoms)
    acc = teacher(
        teacher_nbr.T, nbr_count, features, left, right, ext_pos, w_rad, w_mix, w_out
    )
    ext_rows = (atoms + 2 * G) // L
    grads = acc[:, :ext_rows].reshape(3, atoms + 2 * G)
    above = lax.ppermute(grads[:, :G], AXES, down)
    below = lax.ppermute(grads[:, atoms + G :], AXES, up)
    force = -grads[:, G : atoms + G]
    force = force - jnp.pad(below, ((0, 0), (0, atoms - G))) - jnp.pad(above, ((0, 0), (atoms - G, 0)))
    outgoing = mapping(
        force, atom_bead.reshape(1, atoms), spread(dest), spread(block_start.astype(F32))
    )
    recv = exchange(outgoing)
    bead_force, sums = bead_stage(
        recv, bead_weight.reshape(1, beads), pred, offs, w_first, second, beads * devices
    )
    sums = reduce_all(sums)
    return force, bead_force, pred, sums[:8], sums[8], jnp.sum(sums[9])


def solution(mesh):
    wide = P(None, AXES)
    tall = P(AXES, None)
    flat = P(AXES)
    return jax.shard_map(
        local,
        mesh=mesh,
        in_specs=(
            wide, wide, tall, flat, P(), P(), P(), flat, flat, flat, wide, tall, flat, P(), P(),
        ),
        out_specs=(wide, wide, wide, P(), P(), P()),
        check_vma=False,
    )
```

```python
import functools
import math

import jax
import jax.numpy as jnp
from jax import lax
from jax.experimental import pallas as pl
from jax.experimental.pallas import tpu as pltpu
from jax.sharding import PartitionSpec as P

G = 1024
BPB = 32
BW = 32
K = 12
L = 128
WIN = 24
AXES = ("grp", "brick")
F32 = jnp.float32
BF16 = jnp.bfloat16
RATES = tuple(0.05 * 1.6**b for b in range(8))


def iota(shape, dim):
    return lax.broadcasted_iota(jnp.int32, shape, dim)


def split(x):
    hi = x.astype(BF16).astype(F32)
    return hi, x - hi


def nn(a, b):
    return lax.dot_general(a, b, (((1,), (0,)), ((), ())), preferred_element_type=F32)


def nt(a, b):
    return lax.dot_general(a, b, (((1,), (1,)), ((), ())), preferred_element_type=F32)


def tn(a, b):
    return lax.dot_general(a, b, (((0,), (0,)), ((), ())), preferred_element_type=F32)


def dot3(dot, a, b):
    a_hi, a_lo = (t.astype(BF16) for t in split(a))
    b_hi, b_lo = (t.astype(BF16) for t in split(b))
    return dot(a_hi, b_hi) + dot(a_lo, b_hi) + dot(a_hi, b_lo)


def sigmoid(v):
    return 1.0 / (1.0 + jnp.exp(-v))


def rate_column():
    rows = iota((8, L), 0)
    out = jnp.zeros((8, L), F32)
    for b, rate in enumerate(RATES):
        out = jnp.where(rows == b, rate, out)
    return out


def stack_basis(basis):
    hi, lo = split(basis)
    return jnp.concatenate([hi, lo, hi, jnp.zeros_like(hi)], axis=0)


def stack_weight(weight):
    hi, lo = split(weight)
    return jnp.concatenate([hi, hi, lo, jnp.zeros_like(hi)], axis=0)


PAIR = 2 * L


def forward_part(blk, held, idx_s, idx, count, pos, weights, table):
    rows, slope_w, hots, offs, sent = held
    rel = idx - blk * L
    hi = rel >> 7
    lo16 = (rel & 127).astype(F32).astype(BF16)
    sub16 = iota((L, L), 0).astype(F32).astype(BF16)
    subw = iota((WIN, L), 0)
    one = jnp.ones((), BF16)
    zero = jnp.zeros((), BF16)
    source = jnp.concatenate([pos[j, pl.ds(blk, WIN), :] for j in range(6)], axis=0).astype(BF16)
    own = [pos[c, pl.ds(blk + 8, 1), :] + pos[3 + c, pl.ds(blk + 8, 1), :] for c in range(3)]
    rates = rate_column()
    live = iota((K, L), 0) < count
    found = {}
    radial = {}
    order = iter(range(K * L))
    done = [0]

    def fetch(n, upto=0):
        for _ in range(max(n, upto - done[0])):
            e = next(order, None)
            if e is None:
                return
            done[0] += 1
            rows[pl.ds(e, 1), :] = table[pl.ds(idx_s[0, e], 1), :]

    message = jnp.zeros((L, L), F32)
    pairs = K // 2
    for p in range(pairs + 2):
        if p < pairs:
            pieces = []
            for s in (2 * p, 2 * p + 1):
                pieces.append(jnp.where(sub16 == lo16[s : s + 1, :], one, zero))
                fetch(FETCH)
            hot = jnp.concatenate(pieces, axis=1)
            hots[:, p * PAIR : (p + 1) * PAIR] = hot
            found[p] = nn(source, hot)
            fetch(FETCH)
            yield
        if 0 <= p - 1 < pairs:
            r = p - 1
            bases = []
            for j in range(2):
                s = 2 * r + j
                lanes = slice(j * L, (j + 1) * L)
                mask = subw == hi[s : s + 1, :]
                d = []
                for c in range(3):
                    both = found[r][c * WIN : (c + 1) * WIN, lanes] + found[r][(3 + c) * WIN : (4 + c) * WIN, lanes]
                    d.append(jnp.sum(jnp.where(mask, both, 0.0), axis=0, keepdims=True) - own[c])
                    offs[pl.ds(c * 16 + s, 1), :] = d[c]
                q = d[0] * d[0] + d[1] * d[1] + d[2] * d[2]
                basis = jnp.exp(-rates * q) * jnp.where(live[s : s + 1, :], 1.0, 0.0)
                bases.append(stack_basis(basis))
                fetch(FETCH)
                yield
            both = tn(jnp.concatenate(bases, axis=1).astype(BF16), weights)
            radial[r] = both[:, :L]
            slope_w[r * PAIR : (r + 1) * PAIR, :] = both[:, L:]
            fetch(FETCH)
            yield
        if 0 <= p - 2 < pairs:
            r = p - 2
            fetch(0, (2 * r + 2) * L)
            for j in range(2):
                s = 2 * r + j
                message += radial[r][j * L : (j + 1) * L] * rows[s * L : (s + 1) * L, :]
            yield
    sent[...] = message


def backward_part(blk, own_at, held, idx, mix, w_out, acc, table):
    rows, slope_w, hots, offs, sent = held
    hi = (idx - blk * L) >> 7
    subw = iota((WIN, L), 0)
    mix_hh, mix_l, turn_hh, turn_l = mix
    scale = 1.0 / math.sqrt(K)

    def product(x, w_hh, w_l):
        x_hi, x_lo = split(x)
        wide = jnp.concatenate([x_hi, x_lo], axis=1).astype(BF16)
        return nn(wide, w_hh) + nn(wide[:, :L], w_l)

    own_rows = table[pl.ds(pl.multiple_of(own_at, L), L), :]
    mixed = product(sent[...] * scale, mix_hh, mix_l)
    yield
    pre = mixed + own_rows
    sig = sigmoid(pre)
    up = w_out[...] * (sig * (1.0 + pre * (1.0 - sig)))
    yield
    back = product(up * scale, turn_hh, turn_l)
    yield
    diag = iota((L, L), 0) == iota((L, L), 1)
    own_grad = [jnp.zeros((1, L), F32) for _ in range(3)]
    slopes = {}
    out = None
    pairs = K // 2
    for p in range(pairs + 1):
        if p < pairs:
            for j in range(2):
                s = 2 * p + j
                prod = back * rows[s * L : (s + 1) * L, :] * slope_w[s * L : (s + 1) * L, :]
                summed = jnp.sum(prod, axis=1, keepdims=True)
                slopes[s] = 2.0 * jnp.sum(jnp.where(diag, summed, 0.0), axis=0, keepdims=True)
                yield
        if p >= 1:
            r = p - 1
            parts = [[] for _ in range(6)]
            for s in (2 * r, 2 * r + 1):
                mask = subw == hi[s : s + 1, :]
                for c in range(3):
                    value = slopes[s] * offs[pl.ds(c * 16 + s, 1), :]
                    own_grad[c] -= value
                    v_hi, v_lo = split(value)
                    parts[c].append(jnp.where(mask, v_hi, 0.0))
                    parts[3 + c].append(jnp.where(mask, v_lo, 0.0))
            spread = jnp.concatenate([jnp.concatenate(x, axis=1) for x in parts], axis=0).astype(BF16)
            yield
            got = nt(spread, hots[:, r * PAIR : (r + 1) * PAIR])
            out = got if out is None else out + got
            yield
    for c in range(3):
        both = out[c * WIN : (c + 1) * WIN] + out[(3 + c) * WIN : (4 + c) * WIN]
        both += jnp.where(subw == 8, own_grad[c], 0.0)
        acc[c, pl.ds(blk, WIN), :] += both


FETCH = 40


def run_beside(one, two):
    alive = [one, two]
    while alive:
        for part in list(alive):
            if next(part, 1) == 1:
                alive.remove(part)


EDGE = G // L


def interior_place(blocks, j):
    return j + EDGE, (j + EDGE) * L


def border_place(blocks, j):
    upper = (j >= EDGE).astype(jnp.int32)
    return j + upper * (blocks - 2 * EDGE), G + j * L + upper * 2 * G


def teacher_kernel(sources, place, with_sums, idx_h, idx_v, count_v, pos, w_rad, w_mix, w_out, *rest):
    feats, rest = rest[:sources], rest[sources:]
    if with_sums:
        sums, rest = rest[0], rest[1:]
    acc, table, idx_a, idx_b, sem_a, sem_b = rest[:6]
    held_a, held_b = rest[6:11], rest[11:]
    blocks = idx_h.shape[0]

    def bring(blk, idx, sem):
        return pltpu.make_async_copy(idx_h.at[jnp.minimum(blk, blocks - 1)], idx, sem)

    bring(0, idx_a, sem_a).start()
    bring(1, idx_b, sem_b).start()
    acc[...] = sums[...] if with_sums else jnp.zeros_like(acc)
    base = 0
    for source in feats:
        def one(j, carry, source=source, base=base):
            for u in range(4):
                src = pl.ds(pl.multiple_of(j * 4 * L + u * L, L), L)
                dst = pl.ds(pl.multiple_of(base + j * 4 * L + u * L, L), L)
                table[dst, :] = source[:L, src].T
            return carry

        lax.fori_loop(0, source.shape[1] // (4 * L), one, 0)
        base += source.shape[1]
    weight = w_rad[...]
    rate_w = rate_column() * weight
    weights = jnp.concatenate([stack_weight(weight), stack_weight(-rate_w)], axis=1).astype(BF16)
    mix = []
    for w in (w_mix[...], w_mix[...].T):
        w_hi, w_lo = split(w)
        mix += [jnp.concatenate([w_hi, w_hi], axis=0).astype(BF16), w_lo.astype(BF16)]

    def forward(j, held, idx_s):
        blk, _ = place(j)
        lanes = pl.ds(pl.multiple_of(blk * L, L), L)
        return forward_part(blk, held, idx_s, idx_v[:, lanes], count_v[:, lanes], pos, weights, table)

    def backward(j, held):
        blk, own_at = place(j)
        lanes = pl.ds(pl.multiple_of(blk * L, L), L)
        return backward_part(blk, own_at, held, idx_v[:, lanes], mix, w_out, acc, table)

    bring(0, idx_a, sem_a).wait()
    for _ in forward(jnp.int32(0), held_a, idx_a):
        pass
    bring(2, idx_a, sem_a).start()

    def step(i, carry):
        for t, old, new, idx, sem in ((0, held_a, held_b, idx_b, sem_b), (1, held_b, held_a, idx_a, sem_a)):
            j = 2 * i + t
            bring(j + 1, idx, sem).wait()
            run_beside(backward(j, old), forward(jnp.minimum(j + 1, blocks - 1), new, idx))

            @pl.when(i < blocks // 2 - 1)
            def _():
                bring(j + 3, idx, sem).start()

        return carry

    lax.fori_loop(0, blocks // 2, step, 0)


def teacher_call(name, place, rows_of, idx, count, ext_pos, weights, feats, sums=None):
    atoms = idx.shape[1]
    ext_rows = (atoms + 2 * G) // L
    tall = ext_rows + 24
    pos = jnp.pad(ext_pos.reshape(3, ext_rows, L), ((0, 0), (0, 24), (0, 0)))
    hi = lax.reduce_precision(pos, 8, 7)
    pos = jnp.concatenate([hi, pos - hi], axis=0)
    vmem = pl.BlockSpec(memory_space=pltpu.VMEM)
    whole = lambda x: pl.BlockSpec(x.shape, lambda i: (0,) * x.ndim)
    w_rad, w_mix, w_out = weights
    small = (idx, count.reshape(1, atoms), pos, w_rad, w_mix, w_out.reshape(1, L))
    arrays = [x for x, _ in feats]
    specs = [s if s is not None else whole(x) for x, s in feats]
    width = sum(s.block_shape[1] for s in specs)
    if sums is not None:
        arrays.append(sums)
        specs.append(whole(sums))
    return pl.pallas_call(
        functools.partial(teacher_kernel, len(feats), place, sums is not None),
        grid=(1,),
        in_specs=[pl.BlockSpec(memory_space=pl.ANY)] + [whole(x) for x in small] + specs,
        out_specs=pl.BlockSpec((3, tall, L), lambda i: (0, 0, 0)),
        out_shape=jax.ShapeDtypeStruct((3, tall, L), F32),
        scratch_shapes=[
            pltpu.VMEM((width, L), F32),
            pltpu.SMEM((1, K * L), jnp.int32),
            pltpu.SMEM((1, K * L), jnp.int32),
            pltpu.SemaphoreType.DMA,
            pltpu.SemaphoreType.DMA,
        ]
        + 2
        * [
            pltpu.VMEM((K * L, L), F32),
            pltpu.VMEM((K * L, L), F32),
            pltpu.VMEM((L, K * L), BF16),
            pltpu.VMEM((48, L), F32),
            pltpu.VMEM((L, L), F32),
        ],
        compiler_params=pltpu.CompilerParams(vmem_limit_bytes=52 * 2**20),
        cost_estimate=pl.CostEstimate(
            flops=5 * 10**10, bytes_accessed=64 * 2**20, transcendentals=10**6
        ),
        name=name,
    )(rows_of, *small, *arrays)


def teacher_parts(idx, atoms):
    blocks = atoms // L
    rows = idx.reshape(K, blocks, L).transpose(1, 0, 2).reshape(blocks, 1, K * L)
    inner = rows[EDGE : blocks - EDGE] - G
    outer = jnp.concatenate([rows[:EDGE], rows[blocks - EDGE :] - (atoms - 4 * G)], axis=0)
    return inner, outer


KB = 16


def student_terms(offs, w_first, w2):
    q = offs[0] * offs[0] + offs[1] * offs[1] + offs[2] * offs[2]
    rates = rate_column()
    basis = [jnp.exp(-rates * q[s : s + 1, :]) for s in range(KB)]
    stacked = jnp.concatenate([stack_basis(b) for b in basis], axis=1).astype(BF16)
    z = tn(stack_weight(w_first).astype(BF16), stacked)
    return basis, z


def student_kernel(nbr, pos, w_first, w_second, force, off_out):
    step = pl.program_id(0)
    rel = nbr[...] - step * L
    hi = rel >> 7
    lo = rel & 127
    lane = iota((1, L), 1)
    near = []
    own = []
    for c in range(3):
        first = pos[c, pl.ds(step, 1), :]
        second = pos[c, pl.ds(step + 1, 1), :]
        take = lambda row: jnp.take_along_axis(
            jnp.broadcast_to(row, (KB, L)), lo, axis=1, mode="promise_in_bounds"
        )
        near.append(jnp.where(hi == 0, take(first), take(second)))
        own.append(
            jnp.where(lane < L - BW, pltpu.roll(first, L - BW, 1), pltpu.roll(second, L - BW, 1))
        )
    offs = [near[c] - own[c] for c in range(3)]
    w2 = w_second[...]
    basis, z = student_terms(offs, w_first[...], w2)
    out = [jnp.zeros((1, L), F32) for _ in range(3)]
    for s in range(KB):
        zs = z[:, s * L : (s + 1) * L]
        strength = jnp.sum(w2 * (zs * sigmoid(zs)), axis=0, keepdims=True)
        for c in range(3):
            out[c] += strength * offs[c][s : s + 1, :]
    for c in range(3):
        off_out[c] = offs[c]
        force[pl.ds(c, 1), :] = out[c]


def student(nbr, pos, w_first, w_second):
    beads = nbr.shape[1]
    whole = lambda shape: pl.BlockSpec(shape, lambda i: (0,) * len(shape))
    return pl.pallas_call(
        student_kernel,
        grid=(beads // L,),
        in_specs=[
            pl.BlockSpec((KB, L), lambda i: (0, i)),
            whole(pos.shape),
            whole((8, L)),
            whole((L, 1)),
        ],
        out_specs=[
            pl.BlockSpec((3, L), lambda i: (0, i)),
            pl.BlockSpec((3, KB, L), lambda i: (0, 0, i)),
        ],
        out_shape=[
            jax.ShapeDtypeStruct((3, beads), F32),
            jax.ShapeDtypeStruct((3, KB, beads), F32),
        ],
        compiler_params=pltpu.CompilerParams(vmem_limit_bytes=40 * 2**20),
        cost_estimate=pl.CostEstimate(
            flops=10**9, bytes_accessed=10**6, transcendentals=10**6
        ),
        name="student",
    )(nbr, pos, w_first, w_second)


CHUNK = 1024


def mapping_kernel(force, bead, dest, start, out):
    step = pl.program_id(0)

    @pl.when(step == 0)
    def _():
        out[...] = jnp.zeros_like(out)

    b = bead[...]
    hot = iota((BPB, CHUNK), 0) == b
    highs = []
    lows = []
    for c in range(3):
        hi, lo = split(force[pl.ds(c, 1), :])
        highs.append(jnp.where(hot, hi, 0.0))
        lows.append(jnp.where(hot, lo, 0.0))
    hi, lo = split(start[...])
    first = (iota((BPB, CHUNK), 0) == 0) & (iota((BPB, CHUNK), 1) % 32 == 0)
    highs.append(jnp.where(first, hi, 0.0))
    lows.append(jnp.where(first, lo, 0.0))
    values = jnp.concatenate(highs + lows, axis=0).astype(BF16)
    place = jnp.where(iota((2 * L, CHUNK), 0) == dest[...], 1.0, 0.0).astype(BF16)
    got = nt(place, values)
    out[...] += got[:, :L] + got[:, L:]


def mapping(force, bead, dest, start):
    atoms = force.shape[1]
    row = lambda n: pl.BlockSpec((n, CHUNK), lambda i: (0, i))
    return pl.pallas_call(
        mapping_kernel,
        grid=(atoms // CHUNK,),
        in_specs=[row(3), row(1), row(1), row(1)],
        out_specs=pl.BlockSpec((2 * L, L), lambda i: (0, 0)),
        out_shape=jax.ShapeDtypeStruct((2 * L, L), F32),
        name="mapping",
    )(force, bead, dest, start)


def bead_kernel(beads_all, recv, weight, pred, offs, w_first, w_second, force, out):
    step = pl.program_id(0)
    beads = force.shape[1]

    @pl.when(step == 0)
    def _():
        out[...] = jnp.zeros_like(out)
        turned = jnp.concatenate([recv[:L, :].T, recv[L:, :].T], axis=1)
        start = (turned[96:97, :] + 0.5).astype(jnp.int32)
        hot = jnp.where(iota((beads, 2 * L), 0) == start, 1.0, 0.0).astype(BF16)
        hi, lo = split(turned[:96, :])
        got = nt(jnp.concatenate([hi, lo], axis=0).astype(BF16), hot)
        for c in range(3):
            rows = got[c * BPB : (c + 1) * BPB] + got[96 + c * BPB : 96 + (c + 1) * BPB]
            rows = pltpu.roll(rows, 0, 1, stride=1, stride_axis=0)
            force[pl.ds(c, 1), :] = jnp.sum(rows, axis=0, keepdims=True)

    lanes = pl.ds(pl.multiple_of(step * L, L), L)
    w = weight[...]
    loss = jnp.zeros((1, L), F32)
    pull = []
    for c in range(3):
        res = pred[pl.ds(c, 1), :] - force[pl.ds(c, 1), lanes]
        loss += w * (res * res)
        pull.append((2.0 / (3.0 * beads_all)) * w * res)
    ds = sum(offs[c] * pull[c] for c in range(3))
    rows = jnp.concatenate([ds[s : s + 1, :] for s in range(KB)], axis=1)
    rows_hi, rows_lo = split(rows)
    zeros = jnp.zeros((6, rows.shape[1]), F32)
    second_in = jnp.concatenate([rows_hi, rows_lo, zeros], axis=0).astype(BF16)
    w2 = w_second[...]
    basis, z = student_terms([offs[c] for c in range(3)], w_first[...], w2)
    sig = sigmoid(z)
    slope = w2 * (sig * (1.0 + z * (1.0 - sig)))
    first_hi, first_lo = split(jnp.concatenate(basis, axis=1) * rows)
    first_in = jnp.concatenate([first_hi, first_lo], axis=0).astype(BF16)
    slope_hi, slope_lo = (t.astype(BF16) for t in split(slope))
    hid_hi, hid_lo = (t.astype(BF16) for t in split(z * sig))
    got_hi = nt(first_in, slope_hi)
    got_lo = nt(first_in, slope_lo)
    out[0:8, :] += got_hi[:8] + got_hi[8:] + got_lo[:8]
    two_hi = nt(second_in, hid_hi)
    two_lo = nt(second_in, hid_lo)
    out[8:9, :] += two_hi[0:1] + two_hi[1:2] + two_lo[0:1]
    out[9:10, :] += loss * (1.0 / (3.0 * beads_all))


def bead_stage(recv, weight, pred, offs, w_first, w_second, beads_all):
    beads = pred.shape[1]
    whole = lambda shape: pl.BlockSpec(shape, lambda i: (0,) * len(shape))
    return pl.pallas_call(
        functools.partial(bead_kernel, beads_all),
        grid=(beads // L,),
        in_specs=[
            whole(recv.shape),
            pl.BlockSpec((1, L), lambda i: (0, i)),
            pl.BlockSpec((3, L), lambda i: (0, i)),
            pl.BlockSpec((3, KB, L), lambda i: (0, 0, i)),
            whole((8, L)),
            whole((L, 1)),
        ],
        out_specs=[whole((3, beads)), whole((16, L))],
        out_shape=[
            jax.ShapeDtypeStruct((3, beads), F32),
            jax.ShapeDtypeStruct((16, L), F32),
        ],
        compiler_params=pltpu.CompilerParams(vmem_limit_bytes=40 * 2**20),
        name="beads",
    )(recv, weight, pred, offs, w_first, w_second)


MESH = pl.DeviceIdType.MESH


LOW = 4


def exchange_kernel(src, dst, first, packed, second, send_sem, recv_sem):
    g = lax.axis_index("grp")
    b = lax.axis_index("brick")
    near = lax.axis_size("grp") * LOW
    far = lax.axis_size("brick") // LOW
    h = b // LOW
    z = lax.rem(b, LOW)
    mine = g * LOW + z
    span = 2 * far

    def near_place(d):
        j = lax.rem(mine + d, near)
        return j, (j // LOW, h * LOW + lax.rem(j, LOW))

    def far_place(d):
        j = lax.rem(h + d, far)
        return j, (g, j * LOW + z)

    barrier = pltpu.get_barrier_semaphore()
    for count, place in ((near, near_place), (far, far_place)):
        for d in range(1, count):
            pl.semaphore_signal(barrier, inc=1, device_id=place(d)[1], device_id_type=MESH)
    pl.semaphore_wait(barrier, near + far - 2)
    at_mine = pl.ds(pl.multiple_of(mine * span, span), span)
    copies = []
    for d in range(1, near):
        j, where = near_place(d)
        copies.append(
            pltpu.make_async_remote_copy(
                src_ref=src.at[pl.ds(pl.multiple_of(j * span, span), span)],
                dst_ref=first.at[at_mine],
                send_sem=send_sem.at[d - 1],
                recv_sem=recv_sem.at[d - 1],
                device_id=where,
                device_id_type=MESH,
            )
        )
        copies[-1].start()
    first[at_mine, :] = src[at_mine, :]
    for copy in copies:
        copy.wait()
    for j in range(far):
        packed[j] = first[pl.ds(j, 2 * near, stride=far), :]
    copies = []
    for d in range(1, far):
        j, where = far_place(d)
        copies.append(
            pltpu.make_async_remote_copy(
                src_ref=packed.at[j],
                dst_ref=second.at[h],
                send_sem=send_sem.at[near + d - 2],
                recv_sem=recv_sem.at[near + d - 2],
                device_id=where,
                device_id_type=MESH,
            )
        )
        copies[-1].start()
    second[pl.ds(h, 1)] = packed[pl.ds(h, 1)]
    for copy in copies:
        copy.wait()
    for j in range(far):
        dst[j * 2 * near : (j + 1) * 2 * near, :] = second[j]


def exchange(rows):
    near = lax.axis_size("grp") * LOW
    far = lax.axis_size("brick") // LOW
    vmem = pl.BlockSpec(memory_space=pltpu.VMEM)
    return pl.pallas_call(
        exchange_kernel,
        in_specs=[vmem],
        out_specs=vmem,
        out_shape=jax.ShapeDtypeStruct(rows.shape, F32),
        scratch_shapes=[
            pltpu.VMEM(rows.shape, F32),
            pltpu.VMEM((far, 2 * near, L), F32),
            pltpu.VMEM((far, 2 * near, L), F32),
            pltpu.SemaphoreType.DMA((near + far - 2,)),
            pltpu.SemaphoreType.DMA((near + far - 2,)),
        ],
        compiler_params=pltpu.CompilerParams(collective_id=1, has_side_effects=True),
        name="exchange",
    )(rows)


def reduce_kernel(x, out, first, second, send_sem, recv_sem):
    g = lax.axis_index("grp")
    b = lax.axis_index("brick")
    near = first.shape[0]
    far = second.shape[0]
    z = lax.rem(b, LOW)
    h = b // LOW
    mine = g * LOW + z

    def near_place(d):
        j = lax.rem(mine + d, near)
        return (j // LOW, h * LOW + lax.rem(j, LOW))

    def far_place(d):
        return (g, lax.rem(h + d, far) * LOW + z)

    stages = ((first, near, mine, near_place), (second, far, h, far_place))
    barrier = pltpu.get_barrier_semaphore()
    for _, size, _, where in stages:
        for d in range(1, size):
            pl.semaphore_signal(barrier, inc=1, device_id=where(d), device_id_type=MESH)
    pl.semaphore_wait(barrier, near + far - 2)
    value = x[...]
    used = 0
    for slots, size, at, where in stages:
        slots[pl.ds(at, 1)] = value[None]
        copies = []
        for d in range(1, size):
            copy = pltpu.make_async_remote_copy(
                src_ref=slots.at[at],
                dst_ref=slots.at[at],
                send_sem=send_sem.at[used],
                recv_sem=recv_sem.at[used],
                device_id=where(d),
                device_id_type=MESH,
            )
            used += 1
            copy.start()
            copies.append(copy)
        for copy in copies:
            copy.wait()
        value = slots[0]
        for i in range(1, size):
            value = value + slots[i]
    out[...] = value


def reduce_all(x):
    near = lax.axis_size("grp") * LOW
    far = lax.axis_size("brick") // LOW
    vmem = pl.BlockSpec(memory_space=pltpu.VMEM)
    return pl.pallas_call(
        reduce_kernel,
        in_specs=[vmem],
        out_specs=vmem,
        out_shape=jax.ShapeDtypeStruct(x.shape, F32),
        scratch_shapes=[pltpu.VMEM((n,) + x.shape, F32) for n in (near, far)]
        + [pltpu.SemaphoreType.DMA((near + far - 2,)), pltpu.SemaphoreType.DMA((near + far - 2,))],
        compiler_params=pltpu.CompilerParams(collective_id=2, has_side_effects=True),
        name="reduce",
    )(x)


def local(
    positions,
    features,
    teacher_nbr,
    nbr_count,
    w_rad,
    w_mix,
    w_out,
    block_owner,
    block_start,
    atom_bead,
    bead_pos,
    bead_nbr,
    bead_weight,
    w_first,
    w_second,
):
    atoms = positions.shape[1]
    devices = lax.axis_size(AXES)
    count = devices
    beads = bead_pos.shape[1]
    up = [(i, i + 1) for i in range(count - 1)]
    down = [(i + 1, i) for i in range(count - 1)]

    def payload(feat, pos, bead):
        tail = jnp.concatenate([pos, jnp.pad(bead, ((0, 2), (0, G - BW)))], axis=0)
        return jnp.concatenate([feat, tail], axis=0)

    left = lax.ppermute(
        payload(features[:, atoms - G :], positions[:, atoms - G :], bead_pos[:, beads - BW :]), AXES, up
    )
    right = lax.ppermute(payload(features[:, :G], positions[:, :G], bead_pos[:, :BW]), AXES, down)
    idx = teacher_nbr.T
    inner, outer = teacher_parts(idx, atoms)
    weights = (w_rad, w_mix, w_out)
    blocks_all = atoms // L
    acc = teacher_call(
        "interior", functools.partial(interior_place, blocks_all), inner, idx, nbr_count,
        jnp.pad(positions, ((0, 0), (G, G))), weights, [(features, None)],
    )
    left, right, acc = lax.optimization_barrier((left, right, acc))
    ext_pos = jnp.concatenate([left[L : L + 3], positions, right[L : L + 3]], axis=1)
    bead_ext = jnp.concatenate(
        [left[L + 3 : L + 6, :BW], bead_pos, right[L + 3 : L + 6, :BW], jnp.zeros((3, L - 2 * BW), F32)],
        axis=1,
    )
    second = w_second.reshape(L, 1)
    pred, offs = student(bead_nbr.T, bead_ext.reshape(3, (beads + L) // L, L), w_first, second)
    blocks = block_owner.shape[0]
    block_atoms = atoms // blocks
    order = jnp.arange(blocks, dtype=jnp.int32)
    same = (block_owner[:, None] == block_owner[None, :]) & (order[None, :] < order[:, None])
    rank = jnp.sum(same.astype(jnp.int32), axis=1)
    bricks = lax.axis_size("brick")
    far = bricks // LOW
    near_at = (block_owner // bricks) * LOW + block_owner % LOW
    dest = near_at * 2 * far + rank * far + (block_owner % bricks) // LOW
    spread = lambda v: jnp.broadcast_to(v[:, None], (blocks, block_atoms)).reshape(1, atoms)
    low_feat = pl.BlockSpec((L, 2 * G), lambda i: (0, 0))
    high_feat = pl.BlockSpec((L, 2 * G), lambda i: (0, atoms // (2 * G) - 1))
    acc = teacher_call(
        "border", functools.partial(border_place, blocks_all), outer, idx, nbr_count, ext_pos, weights,
        [(left, None), (features, low_feat), (features, high_feat), (right, None)], acc,
    )
    ext_rows = (atoms + 2 * G) // L
    grads = acc[:, :ext_rows].reshape(3, atoms + 2 * G)
    above = lax.ppermute(grads[:, :G], AXES, down)
    below = lax.ppermute(grads[:, atoms + G :], AXES, up)
    force = -grads[:, G : atoms + G]
    force = force - jnp.pad(below, ((0, 0), (0, atoms - G))) - jnp.pad(above, ((0, 0), (atoms - G, 0)))
    outgoing = mapping(
        force, atom_bead.reshape(1, atoms), spread(dest), spread(block_start.astype(F32))
    )
    recv = exchange(outgoing)
    bead_force, sums = bead_stage(
        recv, bead_weight.reshape(1, beads), pred, offs, w_first, second, beads * devices
    )
    sums = reduce_all(sums)
    return force, bead_force, pred, sums[:8], sums[8], jnp.sum(sums[9])


def solution(mesh):
    wide = P(None, AXES)
    tall = P(AXES, None)
    flat = P(AXES)
    return jax.shard_map(
        local,
        mesh=mesh,
        in_specs=(
            wide, wide, tall, flat, P(), P(), P(), flat, flat, flat, wide, tall, flat, P(), P(),
        ),
        out_specs=(wide, wide, wide, P(), P(), P()),
        check_vma=False,
    )
```

```python
import functools
import math

import jax
import jax.numpy as jnp
from jax import lax
from jax.experimental import pallas as pl
from jax.experimental.pallas import tpu as pltpu
from jax.sharding import PartitionSpec as P

G = 1024
BPB = 32
BW = 32
K = 12
L = 128
WIN = 24
AXES = ("grp", "brick")
F32 = jnp.float32
BF16 = jnp.bfloat16
RATES = tuple(0.05 * 1.6**b for b in range(8))


def iota(shape, dim):
    return lax.broadcasted_iota(jnp.int32, shape, dim)


def split(x):
    hi = x.astype(BF16).astype(F32)
    return hi, x - hi


def nn(a, b):
    return lax.dot_general(a, b, (((1,), (0,)), ((), ())), preferred_element_type=F32)


def nt(a, b):
    return lax.dot_general(a, b, (((1,), (1,)), ((), ())), preferred_element_type=F32)


def tn(a, b):
    return lax.dot_general(a, b, (((0,), (0,)), ((), ())), preferred_element_type=F32)


def dot3(dot, a, b):
    a_hi, a_lo = (t.astype(BF16) for t in split(a))
    b_hi, b_lo = (t.astype(BF16) for t in split(b))
    return dot(a_hi, b_hi) + dot(a_lo, b_hi) + dot(a_hi, b_lo)


def sigmoid(v):
    return 1.0 / (1.0 + jnp.exp(-v))


def rate_column():
    rows = iota((8, L), 0)
    out = jnp.zeros((8, L), F32)
    for b, rate in enumerate(RATES):
        out = jnp.where(rows == b, rate, out)
    return out


def stack_basis(basis):
    hi, lo = split(basis)
    return jnp.concatenate([hi, lo, hi, jnp.zeros_like(hi)], axis=0)


def stack_weight(weight):
    hi, lo = split(weight)
    return jnp.concatenate([hi, hi, lo, jnp.zeros_like(hi)], axis=0)


GF = 4
GB = 4


def forward_part(blk, held, idx_s, idx, count, pos, weights, table):
    rows, slope_w, hots, offs, sent = held
    rel = idx - blk * L
    hi = rel >> 7
    lo16 = (rel & 127).astype(F32).astype(BF16)
    sub16 = iota((L, L), 0).astype(F32).astype(BF16)
    subw = iota((WIN, L), 0)
    one = jnp.ones((), BF16)
    zero = jnp.zeros((), BF16)
    source = jnp.concatenate([pos[j, pl.ds(blk, WIN), :] for j in range(6)], axis=0).astype(BF16)
    own = [pos[c, pl.ds(blk + 8, 1), :] + pos[3 + c, pl.ds(blk + 8, 1), :] for c in range(3)]
    rates = rate_column()
    live = iota((K, L), 0) < count
    found = {}
    radial = {}
    order = iter(range(K * L))
    done = [0]

    def fetch(n, upto=0):
        for _ in range(max(n, upto - done[0])):
            e = next(order, None)
            if e is None:
                return
            done[0] += 1
            rows[pl.ds(e, 1), :] = table[pl.ds(idx_s[0, e], 1), :]

    message = jnp.zeros((L, L), F32)
    pairs = K // GF
    width = GF * L
    for p in range(pairs + 2):
        if p < pairs:
            pieces = []
            for s in range(GF * p, GF * p + GF):
                pieces.append(jnp.where(sub16 == lo16[s : s + 1, :], one, zero))
                fetch(FETCH)
            hot = jnp.concatenate(pieces, axis=1)
            hots[:, p * width : (p + 1) * width] = hot
            found[p] = nn(source, hot)
            fetch(FETCH)
            yield
        if 0 <= p - 1 < pairs:
            r = p - 1
            bases = []
            for j in range(GF):
                s = GF * r + j
                lanes = slice(j * L, (j + 1) * L)
                mask = subw == hi[s : s + 1, :]
                d = []
                for c in range(3):
                    both = found[r][c * WIN : (c + 1) * WIN, lanes] + found[r][(3 + c) * WIN : (4 + c) * WIN, lanes]
                    d.append(jnp.sum(jnp.where(mask, both, 0.0), axis=0, keepdims=True) - own[c])
                    offs[pl.ds(c * 16 + s, 1), :] = d[c]
                q = d[0] * d[0] + d[1] * d[1] + d[2] * d[2]
                basis = jnp.exp(-rates * q) * jnp.where(live[s : s + 1, :], 1.0, 0.0)
                bases.append(stack_basis(basis))
                fetch(FETCH)
                yield
            both = tn(jnp.concatenate(bases, axis=1).astype(BF16), weights)
            radial[r] = both[:, :L]
            slope_w[r * width : (r + 1) * width, :] = both[:, L:]
            fetch(FETCH)
            yield
        if 0 <= p - 2 < pairs:
            r = p - 2
            fetch(0, (r + 1) * width)
            for j in range(GF):
                s = GF * r + j
                message += radial[r][j * L : (j + 1) * L] * rows[s * L : (s + 1) * L, :]
            yield
    sent[...] = message


def backward_part(blk, own_at, held, idx, mix, w_out, acc, table):
    rows, slope_w, hots, offs, sent = held
    hi = (idx - blk * L) >> 7
    subw = iota((WIN, L), 0)
    mix_hh, mix_l, turn_hh, turn_l = mix
    scale = 1.0 / math.sqrt(K)

    def product(x, w_hh, w_l):
        x_hi, x_lo = split(x)
        wide = jnp.concatenate([x_hi, x_lo], axis=1).astype(BF16)
        return nn(wide, w_hh) + nn(wide[:, :L], w_l)

    own_rows = table[pl.ds(pl.multiple_of(own_at, L), L), :]
    mixed = product(sent[...] * scale, mix_hh, mix_l)
    yield
    pre = mixed + own_rows
    sig = sigmoid(pre)
    up = w_out[...] * (sig * (1.0 + pre * (1.0 - sig)))
    yield
    back = product(up * scale, turn_hh, turn_l)
    yield
    diag = iota((L, L), 0) == iota((L, L), 1)
    own_grad = [jnp.zeros((1, L), F32) for _ in range(3)]
    slopes = {}
    out = None
    pairs = K // GB
    width = GB * L
    for p in range(pairs + 1):
        if p < pairs:
            for j in range(GB):
                s = GB * p + j
                prod = back * rows[s * L : (s + 1) * L, :] * slope_w[s * L : (s + 1) * L, :]
                summed = jnp.sum(prod, axis=1, keepdims=True)
                slopes[s] = 2.0 * jnp.sum(jnp.where(diag, summed, 0.0), axis=0, keepdims=True)
                yield
        if p >= 1:
            r = p - 1
            parts = [[] for _ in range(6)]
            for s in range(GB * r, GB * r + GB):
                mask = subw == hi[s : s + 1, :]
                for c in range(3):
                    value = slopes[s] * offs[pl.ds(c * 16 + s, 1), :]
                    own_grad[c] -= value
                    v_hi, v_lo = split(value)
                    parts[c].append(jnp.where(mask, v_hi, 0.0))
                    parts[3 + c].append(jnp.where(mask, v_lo, 0.0))
            spread = jnp.concatenate([jnp.concatenate(x, axis=1) for x in parts], axis=0).astype(BF16)
            yield
            got = nt(spread, hots[:, r * width : (r + 1) * width])
            out = got if out is None else out + got
            yield
    for c in range(3):
        both = out[c * WIN : (c + 1) * WIN] + out[(3 + c) * WIN : (4 + c) * WIN]
        both += jnp.where(subw == 8, own_grad[c], 0.0)
        acc[c, pl.ds(blk, WIN), :] += both


FETCH = 40


def run_beside(one, two):
    alive = [one, two]
    while alive:
        for part in list(alive):
            if next(part, 1) == 1:
                alive.remove(part)


EDGE = G // L


def interior_place(blocks, j):
    return j + EDGE, (j + EDGE) * L


def border_place(blocks, j):
    upper = (j >= EDGE).astype(jnp.int32)
    return j + upper * (blocks - 2 * EDGE), G + j * L + upper * 2 * G


def teacher_kernel(sources, place, with_sums, idx_h, idx_v, count_v, pos, w_rad, w_mix, w_out, *rest):
    feats, rest = rest[:sources], rest[sources:]
    if with_sums:
        sums, rest = rest[0], rest[1:]
    acc, table, idx_a, idx_b, sem_a, sem_b = rest[:6]
    held_a, held_b = rest[6:11], rest[11:]
    blocks = idx_h.shape[0]

    def bring(blk, idx, sem):
        return pltpu.make_async_copy(idx_h.at[jnp.minimum(blk, blocks - 1)], idx, sem)

    bring(0, idx_a, sem_a).start()
    bring(1, idx_b, sem_b).start()
    acc[...] = sums[...] if with_sums else jnp.zeros_like(acc)
    base = 0
    for source in feats:
        def one(j, carry, source=source, base=base):
            for u in range(4):
                src = pl.ds(pl.multiple_of(j * 4 * L + u * L, L), L)
                dst = pl.ds(pl.multiple_of(base + j * 4 * L + u * L, L), L)
                table[dst, :] = source[:L, src].T
            return carry

        lax.fori_loop(0, source.shape[1] // (4 * L), one, 0)
        base += source.shape[1]
    weight = w_rad[...]
    rate_w = rate_column() * weight
    weights = jnp.concatenate([stack_weight(weight), stack_weight(-rate_w)], axis=1).astype(BF16)
    mix = []
    for w in (w_mix[...], w_mix[...].T):
        w_hi, w_lo = split(w)
        mix += [jnp.concatenate([w_hi, w_hi], axis=0).astype(BF16), w_lo.astype(BF16)]

    def forward(j, held, idx_s):
        blk, _ = place(j)
        lanes = pl.ds(pl.multiple_of(blk * L, L), L)
        return forward_part(blk, held, idx_s, idx_v[:, lanes], count_v[:, lanes], pos, weights, table)

    def backward(j, held):
        blk, own_at = place(j)
        lanes = pl.ds(pl.multiple_of(blk * L, L), L)
        return backward_part(blk, own_at, held, idx_v[:, lanes], mix, w_out, acc, table)

    bring(0, idx_a, sem_a).wait()
    for _ in forward(jnp.int32(0), held_a, idx_a):
        pass
    bring(2, idx_a, sem_a).start()

    def step(i, carry):
        for t, old, new, idx, sem in ((0, held_a, held_b, idx_b, sem_b), (1, held_b, held_a, idx_a, sem_a)):
            j = 2 * i + t
            bring(j + 1, idx, sem).wait()
            run_beside(backward(j, old), forward(jnp.minimum(j + 1, blocks - 1), new, idx))

            @pl.when(i < blocks // 2 - 1)
            def _():
                bring(j + 3, idx, sem).start()

        return carry

    lax.fori_loop(0, blocks // 2, step, 0)


def teacher_call(name, place, rows_of, idx, count, ext_pos, weights, feats, sums=None):
    atoms = idx.shape[1]
    ext_rows = (atoms + 2 * G) // L
    tall = ext_rows + 24
    pos = jnp.pad(ext_pos.reshape(3, ext_rows, L), ((0, 0), (0, 24), (0, 0)))
    hi = lax.reduce_precision(pos, 8, 7)
    pos = jnp.concatenate([hi, pos - hi], axis=0)
    vmem = pl.BlockSpec(memory_space=pltpu.VMEM)
    whole = lambda x: pl.BlockSpec(x.shape, lambda i: (0,) * x.ndim)
    w_rad, w_mix, w_out = weights
    small = (idx, count.reshape(1, atoms), pos, w_rad, w_mix, w_out.reshape(1, L))
    arrays = [x for x, _ in feats]
    specs = [s if s is not None else whole(x) for x, s in feats]
    width = sum(s.block_shape[1] for s in specs)
    if sums is not None:
        arrays.append(sums)
        specs.append(whole(sums))
    return pl.pallas_call(
        functools.partial(teacher_kernel, len(feats), place, sums is not None),
        grid=(1,),
        in_specs=[pl.BlockSpec(memory_space=pl.ANY)] + [whole(x) for x in small] + specs,
        out_specs=pl.BlockSpec((3, tall, L), lambda i: (0, 0, 0)),
        out_shape=jax.ShapeDtypeStruct((3, tall, L), F32),
        scratch_shapes=[
            pltpu.VMEM((width, L), F32),
            pltpu.SMEM((1, K * L), jnp.int32),
            pltpu.SMEM((1, K * L), jnp.int32),
            pltpu.SemaphoreType.DMA,
            pltpu.SemaphoreType.DMA,
        ]
        + 2
        * [
            pltpu.VMEM((K * L, L), F32),
            pltpu.VMEM((K * L, L), F32),
            pltpu.VMEM((L, K * L), BF16),
            pltpu.VMEM((48, L), F32),
            pltpu.VMEM((L, L), F32),
        ],
        compiler_params=pltpu.CompilerParams(vmem_limit_bytes=52 * 2**20),
        cost_estimate=pl.CostEstimate(
            flops=5 * 10**10, bytes_accessed=64 * 2**20, transcendentals=10**6
        ),
        name=name,
    )(rows_of, *small, *arrays)


def teacher_parts(idx, atoms):
    blocks = atoms // L
    rows = idx.reshape(K, blocks, L).transpose(1, 0, 2).reshape(blocks, 1, K * L)
    inner = rows[EDGE : blocks - EDGE] - G
    outer = jnp.concatenate([rows[:EDGE], rows[blocks - EDGE :] - (atoms - 4 * G)], axis=0)
    return inner, outer


KB = 16


def student_terms(offs, w_first, w2):
    q = offs[0] * offs[0] + offs[1] * offs[1] + offs[2] * offs[2]
    rates = rate_column()
    basis = [jnp.exp(-rates * q[s : s + 1, :]) for s in range(KB)]
    stacked = jnp.concatenate([stack_basis(b) for b in basis], axis=1).astype(BF16)
    z = tn(stack_weight(w_first).astype(BF16), stacked)
    return basis, z


def student_kernel(nbr, pos, w_first, w_second, force, off_out):
    step = pl.program_id(0)
    rel = nbr[...] - step * L
    hi = rel >> 7
    lo = rel & 127
    lane = iota((1, L), 1)
    near = []
    own = []
    for c in range(3):
        first = pos[c, pl.ds(step, 1), :]
        second = pos[c, pl.ds(step + 1, 1), :]
        take = lambda row: jnp.take_along_axis(
            jnp.broadcast_to(row, (KB, L)), lo, axis=1, mode="promise_in_bounds"
        )
        near.append(jnp.where(hi == 0, take(first), take(second)))
        own.append(
            jnp.where(lane < L - BW, pltpu.roll(first, L - BW, 1), pltpu.roll(second, L - BW, 1))
        )
    offs = [near[c] - own[c] for c in range(3)]
    w2 = w_second[...]
    basis, z = student_terms(offs, w_first[...], w2)
    out = [jnp.zeros((1, L), F32) for _ in range(3)]
    for s in range(KB):
        zs = z[:, s * L : (s + 1) * L]
        strength = jnp.sum(w2 * (zs * sigmoid(zs)), axis=0, keepdims=True)
        for c in range(3):
            out[c] += strength * offs[c][s : s + 1, :]
    for c in range(3):
        off_out[c] = offs[c]
        force[pl.ds(c, 1), :] = out[c]


def student(nbr, pos, w_first, w_second):
    beads = nbr.shape[1]
    whole = lambda shape: pl.BlockSpec(shape, lambda i: (0,) * len(shape))
    return pl.pallas_call(
        student_kernel,
        grid=(beads // L,),
        in_specs=[
            pl.BlockSpec((KB, L), lambda i: (0, i)),
            whole(pos.shape),
            whole((8, L)),
            whole((L, 1)),
        ],
        out_specs=[
            pl.BlockSpec((3, L), lambda i: (0, i)),
            pl.BlockSpec((3, KB, L), lambda i: (0, 0, i)),
        ],
        out_shape=[
            jax.ShapeDtypeStruct((3, beads), F32),
            jax.ShapeDtypeStruct((3, KB, beads), F32),
        ],
        compiler_params=pltpu.CompilerParams(vmem_limit_bytes=40 * 2**20),
        cost_estimate=pl.CostEstimate(
            flops=10**9, bytes_accessed=10**6, transcendentals=10**6
        ),
        name="student",
    )(nbr, pos, w_first, w_second)


CHUNK = 1024


def mapping_kernel(force, bead, dest, start, *rest):
    step = pl.program_id(0)
    out = rest[-1]

    @pl.when(step == 0)
    def _():
        out[...] = rest[0][...] if len(rest) > 1 else jnp.zeros_like(out)

    b = bead[...]
    hot = iota((BPB, CHUNK), 0) == b
    highs = []
    lows = []
    for c in range(3):
        hi, lo = split(force[pl.ds(c, 1), :])
        highs.append(jnp.where(hot, hi, 0.0))
        lows.append(jnp.where(hot, lo, 0.0))
    hi, lo = split(start[...])
    first = (iota((BPB, CHUNK), 0) == 0) & (iota((BPB, CHUNK), 1) % 32 == 0)
    highs.append(jnp.where(first, hi, 0.0))
    lows.append(jnp.where(first, lo, 0.0))
    values = jnp.concatenate(highs + lows, axis=0).astype(BF16)
    place = jnp.where(iota((2 * L, CHUNK), 0) == dest[...], 1.0, 0.0).astype(BF16)
    got = nt(place, values)
    out[...] += got[:, :L] + got[:, L:]


def mapping(force, bead, dest, start, name, count, at, sums=()):
    row = lambda n: pl.BlockSpec((n, CHUNK), lambda i: (0, at(i)))
    flat = pl.BlockSpec((2 * L, L), lambda i: (0, 0))
    return pl.pallas_call(
        mapping_kernel,
        grid=(count,),
        in_specs=[row(3), row(1), row(1), row(1)] + [flat] * len(sums),
        out_specs=flat,
        out_shape=jax.ShapeDtypeStruct((2 * L, L), F32),
        cost_estimate=pl.CostEstimate(
            flops=10**9, bytes_accessed=10**6, transcendentals=0
        ),
        name=name,
    )(force, bead, dest, start, *sums)


def bead_kernel(beads_all, recv, weight, pred, offs, w_first, w_second, force, out):
    step = pl.program_id(0)
    beads = force.shape[1]

    @pl.when(step == 0)
    def _():
        out[...] = jnp.zeros_like(out)
        turned = jnp.concatenate([recv[:L, :].T, recv[L:, :].T], axis=1)
        start = (turned[96:97, :] + 0.5).astype(jnp.int32)
        hot = jnp.where(iota((beads, 2 * L), 0) == start, 1.0, 0.0).astype(BF16)
        hi, lo = split(turned[:96, :])
        got = nt(jnp.concatenate([hi, lo], axis=0).astype(BF16), hot)
        for c in range(3):
            rows = got[c * BPB : (c + 1) * BPB] + got[96 + c * BPB : 96 + (c + 1) * BPB]
            rows = pltpu.roll(rows, 0, 1, stride=1, stride_axis=0)
            force[pl.ds(c, 1), :] = jnp.sum(rows, axis=0, keepdims=True)

    lanes = pl.ds(pl.multiple_of(step * L, L), L)
    w = weight[...]
    loss = jnp.zeros((1, L), F32)
    pull = []
    for c in range(3):
        res = pred[pl.ds(c, 1), :] - force[pl.ds(c, 1), lanes]
        loss += w * (res * res)
        pull.append((2.0 / (3.0 * beads_all)) * w * res)
    ds = sum(offs[c] * pull[c] for c in range(3))
    rows = jnp.concatenate([ds[s : s + 1, :] for s in range(KB)], axis=1)
    rows_hi, rows_lo = split(rows)
    zeros = jnp.zeros((6, rows.shape[1]), F32)
    second_in = jnp.concatenate([rows_hi, rows_lo, zeros], axis=0).astype(BF16)
    w2 = w_second[...]
    basis, z = student_terms([offs[c] for c in range(3)], w_first[...], w2)
    sig = sigmoid(z)
    slope = w2 * (sig * (1.0 + z * (1.0 - sig)))
    first_hi, first_lo = split(jnp.concatenate(basis, axis=1) * rows)
    first_in = jnp.concatenate([first_hi, first_lo], axis=0).astype(BF16)
    slope_hi, slope_lo = (t.astype(BF16) for t in split(slope))
    hid_hi, hid_lo = (t.astype(BF16) for t in split(z * sig))
    got_hi = nt(first_in, slope_hi)
    got_lo = nt(first_in, slope_lo)
    out[0:8, :] += got_hi[:8] + got_hi[8:] + got_lo[:8]
    two_hi = nt(second_in, hid_hi)
    two_lo = nt(second_in, hid_lo)
    out[8:9, :] += two_hi[0:1] + two_hi[1:2] + two_lo[0:1]
    out[9:10, :] += loss * (1.0 / (3.0 * beads_all))


def bead_stage(recv, weight, pred, offs, w_first, w_second, beads_all):
    beads = pred.shape[1]
    whole = lambda shape: pl.BlockSpec(shape, lambda i: (0,) * len(shape))
    return pl.pallas_call(
        functools.partial(bead_kernel, beads_all),
        grid=(beads // L,),
        in_specs=[
            whole(recv.shape),
            pl.BlockSpec((1, L), lambda i: (0, i)),
            pl.BlockSpec((3, L), lambda i: (0, i)),
            pl.BlockSpec((3, KB, L), lambda i: (0, 0, i)),
            whole((8, L)),
            whole((L, 1)),
        ],
        out_specs=[whole((3, beads)), whole((16, L))],
        out_shape=[
            jax.ShapeDtypeStruct((3, beads), F32),
            jax.ShapeDtypeStruct((16, L), F32),
        ],
        compiler_params=pltpu.CompilerParams(vmem_limit_bytes=40 * 2**20),
        name="beads",
    )(recv, weight, pred, offs, w_first, w_second)


MESH = pl.DeviceIdType.MESH


LOW = 4


def exchange_kernel(src, dst, first, packed, second, send_sem, recv_sem):
    g = lax.axis_index("grp")
    b = lax.axis_index("brick")
    near = lax.axis_size("grp") * LOW
    far = lax.axis_size("brick") // LOW
    h = b // LOW
    z = lax.rem(b, LOW)
    mine = g * LOW + z
    span = 2 * far

    def near_place(d):
        j = lax.rem(mine + d, near)
        return j, (j // LOW, h * LOW + lax.rem(j, LOW))

    def far_place(d):
        j = lax.rem(h + d, far)
        return j, (g, j * LOW + z)

    barrier = pltpu.get_barrier_semaphore()
    for count, place in ((near, near_place), (far, far_place)):
        for d in range(1, count):
            pl.semaphore_signal(barrier, inc=1, device_id=place(d)[1], device_id_type=MESH)
    pl.semaphore_wait(barrier, near + far - 2)
    at_mine = pl.ds(pl.multiple_of(mine * span, span), span)
    copies = []
    for d in range(1, near):
        j, where = near_place(d)
        copies.append(
            pltpu.make_async_remote_copy(
                src_ref=src.at[pl.ds(pl.multiple_of(j * span, span), span)],
                dst_ref=first.at[at_mine],
                send_sem=send_sem.at[d - 1],
                recv_sem=recv_sem.at[d - 1],
                device_id=where,
                device_id_type=MESH,
            )
        )
        copies[-1].start()
    first[at_mine, :] = src[at_mine, :]
    for copy in copies:
        copy.wait()
    for j in range(far):
        packed[j] = first[pl.ds(j, 2 * near, stride=far), :]
    copies = []
    for d in range(1, far):
        j, where = far_place(d)
        copies.append(
            pltpu.make_async_remote_copy(
                src_ref=packed.at[j],
                dst_ref=second.at[h],
                send_sem=send_sem.at[near + d - 2],
                recv_sem=recv_sem.at[near + d - 2],
                device_id=where,
                device_id_type=MESH,
            )
        )
        copies[-1].start()
    second[pl.ds(h, 1)] = packed[pl.ds(h, 1)]
    for copy in copies:
        copy.wait()
    for j in range(far):
        dst[j * 2 * near : (j + 1) * 2 * near, :] = second[j]


def exchange(rows):
    near = lax.axis_size("grp") * LOW
    far = lax.axis_size("brick") // LOW
    vmem = pl.BlockSpec(memory_space=pltpu.VMEM)
    return pl.pallas_call(
        exchange_kernel,
        in_specs=[vmem],
        out_specs=vmem,
        out_shape=jax.ShapeDtypeStruct(rows.shape, F32),
        scratch_shapes=[
            pltpu.VMEM(rows.shape, F32),
            pltpu.VMEM((far, 2 * near, L), F32),
            pltpu.VMEM((far, 2 * near, L), F32),
            pltpu.SemaphoreType.DMA((near + far - 2,)),
            pltpu.SemaphoreType.DMA((near + far - 2,)),
        ],
        compiler_params=pltpu.CompilerParams(collective_id=1, has_side_effects=True),
        name="exchange",
    )(rows)


def reduce_kernel(x, out, first, second, send_sem, recv_sem):
    g = lax.axis_index("grp")
    b = lax.axis_index("brick")
    near = first.shape[0]
    far = second.shape[0]
    z = lax.rem(b, LOW)
    h = b // LOW
    mine = g * LOW + z

    def near_place(d):
        j = lax.rem(mine + d, near)
        return (j // LOW, h * LOW + lax.rem(j, LOW))

    def far_place(d):
        return (g, lax.rem(h + d, far) * LOW + z)

    stages = ((first, near, mine, near_place), (second, far, h, far_place))
    barrier = pltpu.get_barrier_semaphore()
    for _, size, _, where in stages:
        for d in range(1, size):
            pl.semaphore_signal(barrier, inc=1, device_id=where(d), device_id_type=MESH)
    pl.semaphore_wait(barrier, near + far - 2)
    value = x[...]
    used = 0
    for slots, size, at, where in stages:
        slots[pl.ds(at, 1)] = value[None]
        copies = []
        for d in range(1, size):
            copy = pltpu.make_async_remote_copy(
                src_ref=slots.at[at],
                dst_ref=slots.at[at],
                send_sem=send_sem.at[used],
                recv_sem=recv_sem.at[used],
                device_id=where(d),
                device_id_type=MESH,
            )
            used += 1
            copy.start()
            copies.append(copy)
        for copy in copies:
            copy.wait()
        value = slots[0]
        for i in range(1, size):
            value = value + slots[i]
    out[...] = value


def reduce_all(x):
    near = lax.axis_size("grp") * LOW
    far = lax.axis_size("brick") // LOW
    vmem = pl.BlockSpec(memory_space=pltpu.VMEM)
    return pl.pallas_call(
        reduce_kernel,
        in_specs=[vmem],
        out_specs=vmem,
        out_shape=jax.ShapeDtypeStruct(x.shape, F32),
        scratch_shapes=[pltpu.VMEM((n,) + x.shape, F32) for n in (near, far)]
        + [pltpu.SemaphoreType.DMA((near + far - 2,)), pltpu.SemaphoreType.DMA((near + far - 2,))],
        compiler_params=pltpu.CompilerParams(collective_id=2, has_side_effects=True),
        name="reduce",
    )(x)


def local(
    positions,
    features,
    teacher_nbr,
    nbr_count,
    w_rad,
    w_mix,
    w_out,
    block_owner,
    block_start,
    atom_bead,
    bead_pos,
    bead_nbr,
    bead_weight,
    w_first,
    w_second,
):
    atoms = positions.shape[1]
    devices = lax.axis_size(AXES)
    count = devices
    beads = bead_pos.shape[1]
    up = [(i, i + 1) for i in range(count - 1)]
    down = [(i + 1, i) for i in range(count - 1)]

    def payload(feat, pos, bead):
        tail = jnp.concatenate([pos, jnp.pad(bead, ((0, 2), (0, G - BW)))], axis=0)
        return jnp.concatenate([feat, tail], axis=0)

    left = lax.ppermute(
        payload(features[:, atoms - G :], positions[:, atoms - G :], bead_pos[:, beads - BW :]), AXES, up
    )
    right = lax.ppermute(payload(features[:, :G], positions[:, :G], bead_pos[:, :BW]), AXES, down)
    idx = teacher_nbr.T
    inner, outer = teacher_parts(idx, atoms)
    weights = (w_rad, w_mix, w_out)
    blocks_all = atoms // L
    acc = teacher_call(
        "interior", functools.partial(interior_place, blocks_all), inner, idx, nbr_count,
        jnp.pad(positions, ((0, 0), (G, G))), weights, [(features, None)],
    )
    left, right, acc = lax.optimization_barrier((left, right, acc))
    ext_pos = jnp.concatenate([left[L : L + 3], positions, right[L : L + 3]], axis=1)
    bead_ext = jnp.concatenate(
        [left[L + 3 : L + 6, :BW], bead_pos, right[L + 3 : L + 6, :BW], jnp.zeros((3, L - 2 * BW), F32)],
        axis=1,
    )
    second = w_second.reshape(L, 1)
    pred, offs = student(bead_nbr.T, bead_ext.reshape(3, (beads + L) // L, L), w_first, second)
    blocks = block_owner.shape[0]
    block_atoms = atoms // blocks
    order = jnp.arange(blocks, dtype=jnp.int32)
    same = (block_owner[:, None] == block_owner[None, :]) & (order[None, :] < order[:, None])
    rank = jnp.sum(same.astype(jnp.int32), axis=1)
    bricks = lax.axis_size("brick")
    far = bricks // LOW
    near_at = (block_owner // bricks) * LOW + block_owner % LOW
    dest = near_at * 2 * far + rank * far + (block_owner % bricks) // LOW
    spread = lambda v: jnp.broadcast_to(v[:, None], (blocks, block_atoms)).reshape(1, atoms)
    low_feat = pl.BlockSpec((L, 2 * G), lambda i: (0, 0))
    high_feat = pl.BlockSpec((L, 2 * G), lambda i: (0, atoms // (2 * G) - 1))
    acc = teacher_call(
        "border", functools.partial(border_place, blocks_all), outer, idx, nbr_count, ext_pos, weights,
        [(left, None), (features, low_feat), (features, high_feat), (right, None)], acc,
    )
    ext_rows = (atoms + 2 * G) // L
    grads = acc[:, :ext_rows].reshape(3, atoms + 2 * G)
    above = lax.ppermute(grads[:, :G], AXES, down)
    below = lax.ppermute(grads[:, atoms + G :], AXES, up)
    raw = -grads[:, G : atoms + G]
    details = (atom_bead.reshape(1, atoms), spread(dest), spread(block_start.astype(F32)))
    last = atoms // CHUNK - 1
    partial = mapping(raw, *details, "mapping_inner", last - 1, lambda i: i + 1)
    above, below, partial = lax.optimization_barrier((above, below, partial))
    force = raw - jnp.pad(below, ((0, 0), (0, atoms - G))) - jnp.pad(above, ((0, 0), (atoms - G, 0)))
    outgoing = mapping(force, *details, "mapping_border", 2, lambda i: i * last, (partial,))
    recv = exchange(outgoing)
    bead_force, sums = bead_stage(
        recv, bead_weight.reshape(1, beads), pred, offs, w_first, second, beads * devices
    )
    sums = reduce_all(sums)
    return force, bead_force, pred, sums[:8], sums[8], jnp.sum(sums[9])


def solution(mesh):
    wide = P(None, AXES)
    tall = P(AXES, None)
    flat = P(AXES)
    return jax.shard_map(
        local,
        mesh=mesh,
        in_specs=(
            wide, wide, tall, flat, P(), P(), P(), flat, flat, flat, wide, tall, flat, P(), P(),
        ),
        out_specs=(wide, wide, wide, P(), P(), P()),
        check_vma=False,
    )
```

```python
import functools
import math

import jax
import jax.numpy as jnp
from jax import lax
from jax.experimental import pallas as pl
from jax.experimental.pallas import tpu as pltpu
from jax.sharding import PartitionSpec as P

G = 1024
BPB = 32
BW = 32
K = 12
L = 128
WIN = 24
AXES = ("grp", "brick")
F32 = jnp.float32
BF16 = jnp.bfloat16
RATES = tuple(0.05 * 1.6**b for b in range(8))


def iota(shape, dim):
    return lax.broadcasted_iota(jnp.int32, shape, dim)


def split(x):
    hi = x.astype(BF16).astype(F32)
    return hi, x - hi


def nn(a, b):
    return lax.dot_general(a, b, (((1,), (0,)), ((), ())), preferred_element_type=F32)


def nt(a, b):
    return lax.dot_general(a, b, (((1,), (1,)), ((), ())), preferred_element_type=F32)


def tn(a, b):
    return lax.dot_general(a, b, (((0,), (0,)), ((), ())), preferred_element_type=F32)


def dot3(dot, a, b):
    a_hi, a_lo = (t.astype(BF16) for t in split(a))
    b_hi, b_lo = (t.astype(BF16) for t in split(b))
    return dot(a_hi, b_hi) + dot(a_lo, b_hi) + dot(a_hi, b_lo)


def sigmoid(v):
    return 1.0 / (1.0 + jnp.exp(-v))


def rate_column():
    rows = iota((8, L), 0)
    out = jnp.zeros((8, L), F32)
    for b, rate in enumerate(RATES):
        out = jnp.where(rows == b, rate, out)
    return out


def stack_basis(basis):
    hi, lo = split(basis)
    return jnp.concatenate([hi, lo, hi, jnp.zeros_like(hi)], axis=0)


def stack_weight(weight):
    hi, lo = split(weight)
    return jnp.concatenate([hi, hi, lo, jnp.zeros_like(hi)], axis=0)


GF = 4
GB = 4


def forward_part(blk, held, idx_s, idx, count, pos, weights, table):
    rows, slope_w, hots, offs, sent = held
    rel = idx - blk * L
    hi = rel >> 7
    lo16 = (rel & 127).astype(F32).astype(BF16)
    sub16 = iota((L, L), 0).astype(F32).astype(BF16)
    subw = iota((WIN, L), 0)
    one = jnp.ones((), BF16)
    zero = jnp.zeros((), BF16)
    source = jnp.concatenate([pos[j, pl.ds(blk, WIN), :] for j in range(6)], axis=0).astype(BF16)
    own = [pos[c, pl.ds(blk + 8, 1), :] + pos[3 + c, pl.ds(blk + 8, 1), :] for c in range(3)]
    rates = rate_column()
    live = iota((K, L), 0) < count
    found = {}
    radial = {}
    order = iter(range(K * L))
    done = [0]

    def fetch(n, upto=0):
        for _ in range(max(n, upto - done[0])):
            e = next(order, None)
            if e is None:
                return
            done[0] += 1
            rows[pl.ds(e, 1), :] = table[pl.ds(idx_s[0, e], 1), :]

    message = jnp.zeros((L, L), F32)
    pairs = K // GF
    width = GF * L
    for p in range(pairs + 2):
        if p < pairs:
            pieces = []
            for s in range(GF * p, GF * p + GF):
                pieces.append(jnp.where(sub16 == lo16[s : s + 1, :], one, zero))
                fetch(FETCH)
            hot = jnp.concatenate(pieces, axis=1)
            hots[:, p * width : (p + 1) * width] = hot
            found[p] = nn(source, hot)
            fetch(FETCH)
            yield
        if 0 <= p - 1 < pairs:
            r = p - 1
            bases = []
            for j in range(GF):
                s = GF * r + j
                lanes = slice(j * L, (j + 1) * L)
                mask = subw == hi[s : s + 1, :]
                d = []
                for c in range(3):
                    both = found[r][c * WIN : (c + 1) * WIN, lanes] + found[r][(3 + c) * WIN : (4 + c) * WIN, lanes]
                    d.append(jnp.sum(jnp.where(mask, both, 0.0), axis=0, keepdims=True) - own[c])
                    offs[pl.ds(c * 16 + s, 1), :] = d[c]
                q = d[0] * d[0] + d[1] * d[1] + d[2] * d[2]
                basis = jnp.exp(-rates * q) * jnp.where(live[s : s + 1, :], 1.0, 0.0)
                bases.append(stack_basis(basis))
                fetch(FETCH)
                yield
            both = tn(jnp.concatenate(bases, axis=1).astype(BF16), weights)
            radial[r] = both[:, :L]
            slope_w[r * width : (r + 1) * width, :] = both[:, L:]
            fetch(FETCH)
            yield
        if 0 <= p - 2 < pairs:
            r = p - 2
            fetch(0, (r + 1) * width)
            for j in range(GF):
                s = GF * r + j
                message += radial[r][j * L : (j + 1) * L] * rows[s * L : (s + 1) * L, :]
            yield
    sent[...] = message


def backward_part(blk, own_at, held, idx, mix, w_out, acc, table):
    rows, slope_w, hots, offs, sent = held
    hi = (idx - blk * L) >> 7
    subw = iota((WIN, L), 0)
    mix_hh, mix_l, turn_hh, turn_l = mix
    scale = 1.0 / math.sqrt(K)

    def product(x, w_hh, w_l):
        x_hi, x_lo = split(x)
        wide = jnp.concatenate([x_hi, x_lo], axis=1).astype(BF16)
        return nn(wide, w_hh) + nn(wide[:, :L], w_l)

    own_rows = table[pl.ds(pl.multiple_of(own_at, L), L), :]
    mixed = product(sent[...] * scale, mix_hh, mix_l)
    yield
    pre = mixed + own_rows
    sig = sigmoid(pre)
    up = w_out[...] * (sig * (1.0 + pre * (1.0 - sig)))
    yield
    back = product(up * scale, turn_hh, turn_l)
    yield
    diag = iota((L, L), 0) == iota((L, L), 1)
    own_grad = [jnp.zeros((1, L), F32) for _ in range(3)]
    slopes = {}
    out = None
    pairs = K // GB
    width = GB * L
    for p in range(pairs + 1):
        if p < pairs:
            for j in range(GB):
                s = GB * p + j
                prod = back * rows[s * L : (s + 1) * L, :] * slope_w[s * L : (s + 1) * L, :]
                summed = jnp.sum(prod, axis=1, keepdims=True)
                slopes[s] = 2.0 * jnp.sum(jnp.where(diag, summed, 0.0), axis=0, keepdims=True)
                yield
        if p >= 1:
            r = p - 1
            parts = [[] for _ in range(6)]
            for s in range(GB * r, GB * r + GB):
                mask = subw == hi[s : s + 1, :]
                for c in range(3):
                    value = slopes[s] * offs[pl.ds(c * 16 + s, 1), :]
                    own_grad[c] -= value
                    v_hi, v_lo = split(value)
                    parts[c].append(jnp.where(mask, v_hi, 0.0))
                    parts[3 + c].append(jnp.where(mask, v_lo, 0.0))
            spread = jnp.concatenate([jnp.concatenate(x, axis=1) for x in parts], axis=0).astype(BF16)
            yield
            got = nt(spread, hots[:, r * width : (r + 1) * width])
            out = got if out is None else out + got
            yield
    for c in range(3):
        both = out[c * WIN : (c + 1) * WIN] + out[(3 + c) * WIN : (4 + c) * WIN]
        both += jnp.where(subw == 8, own_grad[c], 0.0)
        acc[c, pl.ds(blk, WIN), :] += both


FETCH = 40


def run_beside(one, two):
    alive = [one, two]
    while alive:
        for part in list(alive):
            if next(part, 1) == 1:
                alive.remove(part)


EDGE = G // L


def interior_place(blocks, j):
    return j + EDGE, (j + EDGE) * L


def border_place(blocks, j):
    upper = (j >= EDGE).astype(jnp.int32)
    return j + upper * (blocks - 2 * EDGE), G + j * L + upper * 2 * G


def teacher_kernel(sources, place, with_sums, idx_h, idx_v, count_v, pos, w_rad, w_mix, w_out, *rest):
    feats, rest = rest[:sources], rest[sources:]
    if with_sums:
        sums, rest = rest[0], rest[1:]
    acc, table, idx_a, idx_b, sem_a, sem_b = rest[:6]
    held_a, held_b = rest[6:11], rest[11:]
    blocks = idx_h.shape[0]

    def bring(blk, idx, sem):
        return pltpu.make_async_copy(idx_h.at[jnp.minimum(blk, blocks - 1)], idx, sem)

    bring(0, idx_a, sem_a).start()
    bring(1, idx_b, sem_b).start()
    acc[...] = sums[...] if with_sums else jnp.zeros_like(acc)
    base = 0
    for source in feats:
        def one(j, carry, source=source, base=base):
            for u in range(4):
                src = pl.ds(pl.multiple_of(j * 4 * L + u * L, L), L)
                dst = pl.ds(pl.multiple_of(base + j * 4 * L + u * L, L), L)
                table[dst, :] = source[:L, src].T
            return carry

        lax.fori_loop(0, source.shape[1] // (4 * L), one, 0)
        base += source.shape[1]
    weight = w_rad[...]
    rate_w = rate_column() * weight
    weights = jnp.concatenate([stack_weight(weight), stack_weight(-rate_w)], axis=1).astype(BF16)
    mix = []
    for w in (w_mix[...], w_mix[...].T):
        w_hi, w_lo = split(w)
        mix += [jnp.concatenate([w_hi, w_hi], axis=0).astype(BF16), w_lo.astype(BF16)]

    def forward(j, held, idx_s):
        blk, _ = place(j)
        lanes = pl.ds(pl.multiple_of(blk * L, L), L)
        return forward_part(blk, held, idx_s, idx_v[:, lanes], count_v[:, lanes], pos, weights, table)

    def backward(j, held):
        blk, own_at = place(j)
        lanes = pl.ds(pl.multiple_of(blk * L, L), L)
        return backward_part(blk, own_at, held, idx_v[:, lanes], mix, w_out, acc, table)

    bring(0, idx_a, sem_a).wait()
    for _ in forward(jnp.int32(0), held_a, idx_a):
        pass
    bring(2, idx_a, sem_a).start()

    def step(i, carry):
        for t, old, new, idx, sem in ((0, held_a, held_b, idx_b, sem_b), (1, held_b, held_a, idx_a, sem_a)):
            j = 2 * i + t
            bring(j + 1, idx, sem).wait()
            run_beside(backward(j, old), forward(jnp.minimum(j + 1, blocks - 1), new, idx))

            @pl.when(i < blocks // 2 - 1)
            def _():
                bring(j + 3, idx, sem).start()

        return carry

    lax.fori_loop(0, blocks // 2, step, 0)


def teacher_call(name, place, rows_of, idx, count, ext_pos, weights, feats, sums=None):
    atoms = idx.shape[1]
    ext_rows = (atoms + 2 * G) // L
    tall = ext_rows + 24
    pos = jnp.pad(ext_pos.reshape(3, ext_rows, L), ((0, 0), (0, 24), (0, 0)))
    hi = lax.reduce_precision(pos, 8, 7)
    pos = jnp.concatenate([hi, pos - hi], axis=0)
    vmem = pl.BlockSpec(memory_space=pltpu.VMEM)
    whole = lambda x: pl.BlockSpec(x.shape, lambda i: (0,) * x.ndim)
    w_rad, w_mix, w_out = weights
    small = (idx, count.reshape(1, atoms), pos, w_rad, w_mix, w_out.reshape(1, L))
    arrays = [x for x, _ in feats]
    specs = [s if s is not None else whole(x) for x, s in feats]
    width = sum(s.block_shape[1] for s in specs)
    if sums is not None:
        arrays.append(sums)
        specs.append(whole(sums))
    return pl.pallas_call(
        functools.partial(teacher_kernel, len(feats), place, sums is not None),
        grid=(1,),
        in_specs=[pl.BlockSpec(memory_space=pl.ANY)] + [whole(x) for x in small] + specs,
        out_specs=pl.BlockSpec((3, tall, L), lambda i: (0, 0, 0)),
        out_shape=jax.ShapeDtypeStruct((3, tall, L), F32),
        scratch_shapes=[
            pltpu.VMEM((width, L), F32),
            pltpu.SMEM((1, K * L), jnp.int32),
            pltpu.SMEM((1, K * L), jnp.int32),
            pltpu.SemaphoreType.DMA,
            pltpu.SemaphoreType.DMA,
        ]
        + 2
        * [
            pltpu.VMEM((K * L, L), F32),
            pltpu.VMEM((K * L, L), F32),
            pltpu.VMEM((L, K * L), BF16),
            pltpu.VMEM((48, L), F32),
            pltpu.VMEM((L, L), F32),
        ],
        compiler_params=pltpu.CompilerParams(vmem_limit_bytes=52 * 2**20),
        cost_estimate=pl.CostEstimate(
            flops=5 * 10**10, bytes_accessed=64 * 2**20, transcendentals=10**6
        ),
        name=name,
    )(rows_of, *small, *arrays)


def teacher_parts(idx, atoms):
    blocks = atoms // L
    rows = idx.reshape(K, blocks, L).transpose(1, 0, 2).reshape(blocks, 1, K * L)
    inner = rows[EDGE : blocks - EDGE] - G
    outer = jnp.concatenate([rows[:EDGE], rows[blocks - EDGE :] - (atoms - 4 * G)], axis=0)
    return inner, outer


KB = 16


def student_terms(offs, w_first, w2):
    q = offs[0] * offs[0] + offs[1] * offs[1] + offs[2] * offs[2]
    rates = rate_column()
    basis = [jnp.exp(-rates * q[s : s + 1, :]) for s in range(KB)]
    stacked = jnp.concatenate([stack_basis(b) for b in basis], axis=1).astype(BF16)
    z = tn(stack_weight(w_first).astype(BF16), stacked)
    return basis, z


def student_kernel(nbr, pos, w_first, w_second, force, off_out):
    step = pl.program_id(0)
    rel = nbr[...] - step * L
    hi = rel >> 7
    lo = rel & 127
    lane = iota((1, L), 1)
    near = []
    own = []
    for c in range(3):
        first = pos[c, pl.ds(step, 1), :]
        second = pos[c, pl.ds(step + 1, 1), :]
        take = lambda row: jnp.take_along_axis(
            jnp.broadcast_to(row, (KB, L)), lo, axis=1, mode="promise_in_bounds"
        )
        near.append(jnp.where(hi == 0, take(first), take(second)))
        own.append(
            jnp.where(lane < L - BW, pltpu.roll(first, L - BW, 1), pltpu.roll(second, L - BW, 1))
        )
    offs = [near[c] - own[c] for c in range(3)]
    w2 = w_second[...]
    basis, z = student_terms(offs, w_first[...], w2)
    out = [jnp.zeros((1, L), F32) for _ in range(3)]
    for s in range(KB):
        zs = z[:, s * L : (s + 1) * L]
        strength = jnp.sum(w2 * (zs * sigmoid(zs)), axis=0, keepdims=True)
        for c in range(3):
            out[c] += strength * offs[c][s : s + 1, :]
    for c in range(3):
        off_out[c] = offs[c]
        force[pl.ds(c, 1), :] = out[c]


def student(nbr, pos, w_first, w_second):
    beads = nbr.shape[1]
    whole = lambda shape: pl.BlockSpec(shape, lambda i: (0,) * len(shape))
    return pl.pallas_call(
        student_kernel,
        grid=(beads // L,),
        in_specs=[
            pl.BlockSpec((KB, L), lambda i: (0, i)),
            whole(pos.shape),
            whole((8, L)),
            whole((L, 1)),
        ],
        out_specs=[
            pl.BlockSpec((3, L), lambda i: (0, i)),
            pl.BlockSpec((3, KB, L), lambda i: (0, 0, i)),
        ],
        out_shape=[
            jax.ShapeDtypeStruct((3, beads), F32),
            jax.ShapeDtypeStruct((3, KB, beads), F32),
        ],
        compiler_params=pltpu.CompilerParams(vmem_limit_bytes=40 * 2**20),
        cost_estimate=pl.CostEstimate(
            flops=10**9, bytes_accessed=10**6, transcendentals=10**6
        ),
        name="student",
    )(nbr, pos, w_first, w_second)


CHUNK = 1024


def mapping_kernel(force, bead, dest, start, *rest):
    step = pl.program_id(0)
    out = rest[-1]

    @pl.when(step == 0)
    def _():
        out[...] = rest[0][...] if len(rest) > 1 else jnp.zeros_like(out)

    b = bead[...]
    hot = iota((BPB, CHUNK), 0) == b
    highs = []
    lows = []
    for c in range(3):
        hi, lo = split(force[pl.ds(c, 1), :])
        highs.append(jnp.where(hot, hi, 0.0))
        lows.append(jnp.where(hot, lo, 0.0))
    hi, lo = split(start[...])
    first = (iota((BPB, CHUNK), 0) == 0) & (iota((BPB, CHUNK), 1) % 32 == 0)
    highs.append(jnp.where(first, hi, 0.0))
    lows.append(jnp.where(first, lo, 0.0))
    values = jnp.concatenate(highs + lows, axis=0).astype(BF16)
    place = jnp.where(iota((2 * L, CHUNK), 0) == dest[...], 1.0, 0.0).astype(BF16)
    got = nt(place, values)
    out[...] += got[:, :L] + got[:, L:]


def mapping(force, bead, dest, start, name, count, at, sums=()):
    row = lambda n: pl.BlockSpec((n, CHUNK), lambda i: (0, at(i)))
    flat = pl.BlockSpec((2 * L, L), lambda i: (0, 0))
    return pl.pallas_call(
        mapping_kernel,
        grid=(count,),
        in_specs=[row(3), row(1), row(1), row(1)] + [flat] * len(sums),
        out_specs=flat,
        out_shape=jax.ShapeDtypeStruct((2 * L, L), F32),
        cost_estimate=pl.CostEstimate(
            flops=10**9, bytes_accessed=10**6, transcendentals=0
        ),
        name=name,
    )(force, bead, dest, start, *sums)


def bead_kernel(beads_all, recv, weight, pred, offs, w_first, w_second, force, out):
    step = pl.program_id(0)
    beads = force.shape[1]

    @pl.when(step == 0)
    def _():
        out[...] = jnp.zeros_like(out)
        turned = jnp.concatenate([recv[:L, :].T, recv[L:, :].T], axis=1)
        start = (turned[96:97, :] + 0.5).astype(jnp.int32)
        hot = jnp.where(iota((beads, 2 * L), 0) == start, 1.0, 0.0).astype(BF16)
        hi, lo = split(turned[:96, :])
        got = nt(jnp.concatenate([hi, lo], axis=0).astype(BF16), hot)
        for c in range(3):
            rows = got[c * BPB : (c + 1) * BPB] + got[96 + c * BPB : 96 + (c + 1) * BPB]
            rows = pltpu.roll(rows, 0, 1, stride=1, stride_axis=0)
            force[pl.ds(c, 1), :] = jnp.sum(rows, axis=0, keepdims=True)

    lanes = pl.ds(pl.multiple_of(step * L, L), L)
    w = weight[...]
    loss = jnp.zeros((1, L), F32)
    pull = []
    for c in range(3):
        res = pred[pl.ds(c, 1), :] - force[pl.ds(c, 1), lanes]
        loss += w * (res * res)
        pull.append((2.0 / (3.0 * beads_all)) * w * res)
    ds = sum(offs[c] * pull[c] for c in range(3))
    rows = jnp.concatenate([ds[s : s + 1, :] for s in range(KB)], axis=1)
    rows_hi, rows_lo = split(rows)
    zeros = jnp.zeros((6, rows.shape[1]), F32)
    second_in = jnp.concatenate([rows_hi, rows_lo, zeros], axis=0).astype(BF16)
    w2 = w_second[...]
    basis, z = student_terms([offs[c] for c in range(3)], w_first[...], w2)
    sig = sigmoid(z)
    slope = w2 * (sig * (1.0 + z * (1.0 - sig)))
    first_hi, first_lo = split(jnp.concatenate(basis, axis=1) * rows)
    first_in = jnp.concatenate([first_hi, first_lo], axis=0).astype(BF16)
    slope_hi, slope_lo = (t.astype(BF16) for t in split(slope))
    hid_hi, hid_lo = (t.astype(BF16) for t in split(z * sig))
    got_hi = nt(first_in, slope_hi)
    got_lo = nt(first_in, slope_lo)
    out[0:8, :] += got_hi[:8] + got_hi[8:] + got_lo[:8]
    two_hi = nt(second_in, hid_hi)
    two_lo = nt(second_in, hid_lo)
    out[8:9, :] += two_hi[0:1] + two_hi[1:2] + two_lo[0:1]
    out[9:10, :] += loss * (1.0 / (3.0 * beads_all))


def bead_stage(recv, weight, pred, offs, w_first, w_second, beads_all):
    beads = pred.shape[1]
    whole = lambda shape: pl.BlockSpec(shape, lambda i: (0,) * len(shape))
    return pl.pallas_call(
        functools.partial(bead_kernel, beads_all),
        grid=(beads // L,),
        in_specs=[
            whole(recv.shape),
            pl.BlockSpec((1, L), lambda i: (0, i)),
            pl.BlockSpec((3, L), lambda i: (0, i)),
            pl.BlockSpec((3, KB, L), lambda i: (0, 0, i)),
            whole((8, L)),
            whole((L, 1)),
        ],
        out_specs=[whole((3, beads)), whole((16, L))],
        out_shape=[
            jax.ShapeDtypeStruct((3, beads), F32),
            jax.ShapeDtypeStruct((16, L), F32),
        ],
        compiler_params=pltpu.CompilerParams(vmem_limit_bytes=40 * 2**20),
        name="beads",
    )(recv, weight, pred, offs, w_first, w_second)


MESH = pl.DeviceIdType.MESH


LOW = 4


def exchange_kernel(src, dst, first, packed, second, send_sem, recv_sem):
    g = lax.axis_index("grp")
    b = lax.axis_index("brick")
    near = lax.axis_size("grp") * LOW
    far = lax.axis_size("brick") // LOW
    h = b // LOW
    z = lax.rem(b, LOW)
    mine = g * LOW + z
    span = 2 * far

    def near_place(d):
        j = lax.rem(mine + d, near)
        return j, (j // LOW, h * LOW + lax.rem(j, LOW))

    def far_place(d):
        j = lax.rem(h + d, far)
        return j, (g, j * LOW + z)

    barrier = pltpu.get_barrier_semaphore()
    for count, place in ((near, near_place), (far, far_place)):
        for d in range(1, count):
            pl.semaphore_signal(barrier, inc=1, device_id=place(d)[1], device_id_type=MESH)
    pl.semaphore_wait(barrier, near + far - 2)
    at_mine = pl.ds(pl.multiple_of(mine * span, span), span)
    copies = []
    for d in range(1, near):
        j, where = near_place(d)
        copies.append(
            pltpu.make_async_remote_copy(
                src_ref=src.at[pl.ds(pl.multiple_of(j * span, span), span)],
                dst_ref=first.at[at_mine],
                send_sem=send_sem.at[d - 1],
                recv_sem=recv_sem.at[d - 1],
                device_id=where,
                device_id_type=MESH,
            )
        )
        copies[-1].start()
    first[at_mine, :] = src[at_mine, :]
    for copy in copies:
        copy.wait()
    for j in range(far):
        packed[j] = first[pl.ds(j, 2 * near, stride=far), :]
    copies = []
    for d in range(1, far):
        j, where = far_place(d)
        copies.append(
            pltpu.make_async_remote_copy(
                src_ref=packed.at[j],
                dst_ref=second.at[h],
                send_sem=send_sem.at[near + d - 2],
                recv_sem=recv_sem.at[near + d - 2],
                device_id=where,
                device_id_type=MESH,
            )
        )
        copies[-1].start()
    second[pl.ds(h, 1)] = packed[pl.ds(h, 1)]
    for copy in copies:
        copy.wait()
    for j in range(far):
        dst[j * 2 * near : (j + 1) * 2 * near, :] = second[j]


def exchange(rows):
    near = lax.axis_size("grp") * LOW
    far = lax.axis_size("brick") // LOW
    vmem = pl.BlockSpec(memory_space=pltpu.VMEM)
    return pl.pallas_call(
        exchange_kernel,
        in_specs=[vmem],
        out_specs=vmem,
        out_shape=jax.ShapeDtypeStruct(rows.shape, F32),
        scratch_shapes=[
            pltpu.VMEM(rows.shape, F32),
            pltpu.VMEM((far, 2 * near, L), F32),
            pltpu.VMEM((far, 2 * near, L), F32),
            pltpu.SemaphoreType.DMA((near + far - 2,)),
            pltpu.SemaphoreType.DMA((near + far - 2,)),
        ],
        compiler_params=pltpu.CompilerParams(collective_id=1, has_side_effects=True),
        name="exchange",
    )(rows)


def reduce_kernel(x, grad_one, grad_two, loss, first, second, send_sem, recv_sem):
    g = lax.axis_index("grp")
    b = lax.axis_index("brick")
    near = first.shape[0]
    far = second.shape[0]
    z = lax.rem(b, LOW)
    h = b // LOW
    mine = g * LOW + z

    def near_place(d):
        j = lax.rem(mine + d, near)
        return (j // LOW, h * LOW + lax.rem(j, LOW))

    def far_place(d):
        return (g, lax.rem(h + d, far) * LOW + z)

    stages = ((first, near, mine, near_place), (second, far, h, far_place))
    barrier = pltpu.get_barrier_semaphore()
    for _, size, _, where in stages:
        for d in range(1, size):
            pl.semaphore_signal(barrier, inc=1, device_id=where(d), device_id_type=MESH)
    pl.semaphore_wait(barrier, near + far - 2)
    value = x[...]
    used = 0
    for slots, size, at, where in stages:
        slots[pl.ds(at, 1)] = value[None]
        copies = []
        for d in range(1, size):
            copy = pltpu.make_async_remote_copy(
                src_ref=slots.at[at],
                dst_ref=slots.at[at],
                send_sem=send_sem.at[used],
                recv_sem=recv_sem.at[used],
                device_id=where(d),
                device_id_type=MESH,
            )
            used += 1
            copy.start()
            copies.append(copy)
        for copy in copies:
            copy.wait()
        value = slots[0]
        for i in range(1, size):
            value = value + slots[i]
    grad_one[...] = value[:8]
    grad_two[...] = value[8:9]
    loss[...] = jnp.sum(value[9:10], axis=1, keepdims=True)


def reduce_all(x):
    near = lax.axis_size("grp") * LOW
    far = lax.axis_size("brick") // LOW
    vmem = pl.BlockSpec(memory_space=pltpu.VMEM)
    return pl.pallas_call(
        reduce_kernel,
        in_specs=[vmem],
        out_specs=[vmem] * 3,
        out_shape=[jax.ShapeDtypeStruct(s, F32) for s in ((8, L), (1, L), (1, 1))],
        scratch_shapes=[pltpu.VMEM((n,) + x.shape, F32) for n in (near, far)]
        + [pltpu.SemaphoreType.DMA((near + far - 2,)), pltpu.SemaphoreType.DMA((near + far - 2,))],
        compiler_params=pltpu.CompilerParams(collective_id=2, has_side_effects=True),
        name="reduce",
    )(x)


def local(
    positions,
    features,
    teacher_nbr,
    nbr_count,
    w_rad,
    w_mix,
    w_out,
    block_owner,
    block_start,
    atom_bead,
    bead_pos,
    bead_nbr,
    bead_weight,
    w_first,
    w_second,
):
    atoms = positions.shape[1]
    devices = lax.axis_size(AXES)
    count = devices
    beads = bead_pos.shape[1]
    up = [(i, i + 1) for i in range(count - 1)]
    down = [(i + 1, i) for i in range(count - 1)]

    def payload(feat, pos, bead):
        tail = jnp.concatenate([pos, jnp.pad(bead, ((0, 2), (0, G - BW)))], axis=0)
        return jnp.concatenate([feat, tail], axis=0)

    left = lax.ppermute(
        payload(features[:, atoms - G :], positions[:, atoms - G :], bead_pos[:, beads - BW :]), AXES, up
    )
    right = lax.ppermute(payload(features[:, :G], positions[:, :G], bead_pos[:, :BW]), AXES, down)
    idx = teacher_nbr.T
    inner, outer = teacher_parts(idx, atoms)
    weights = (w_rad, w_mix, w_out)
    blocks_all = atoms // L
    acc = teacher_call(
        "interior", functools.partial(interior_place, blocks_all), inner, idx, nbr_count,
        jnp.pad(positions, ((0, 0), (G, G))), weights, [(features, None)],
    )
    left, right, acc = lax.optimization_barrier((left, right, acc))
    ext_pos = jnp.concatenate([left[L : L + 3], positions, right[L : L + 3]], axis=1)
    bead_ext = jnp.concatenate(
        [left[L + 3 : L + 6, :BW], bead_pos, right[L + 3 : L + 6, :BW], jnp.zeros((3, L - 2 * BW), F32)],
        axis=1,
    )
    second = w_second.reshape(L, 1)
    pred, offs = student(bead_nbr.T, bead_ext.reshape(3, (beads + L) // L, L), w_first, second)
    blocks = block_owner.shape[0]
    block_atoms = atoms // blocks
    order = jnp.arange(blocks, dtype=jnp.int32)
    same = (block_owner[:, None] == block_owner[None, :]) & (order[None, :] < order[:, None])
    rank = jnp.sum(same.astype(jnp.int32), axis=1)
    bricks = lax.axis_size("brick")
    far = bricks // LOW
    near_at = (block_owner // bricks) * LOW + block_owner % LOW
    dest = near_at * 2 * far + rank * far + (block_owner % bricks) // LOW
    spread = lambda v: jnp.broadcast_to(v[:, None], (blocks, block_atoms)).reshape(1, atoms)
    low_feat = pl.BlockSpec((L, 2 * G), lambda i: (0, 0))
    high_feat = pl.BlockSpec((L, 2 * G), lambda i: (0, atoms // (2 * G) - 1))
    acc = teacher_call(
        "border", functools.partial(border_place, blocks_all), outer, idx, nbr_count, ext_pos, weights,
        [(left, None), (features, low_feat), (features, high_feat), (right, None)], acc,
    )
    ext_rows = (atoms + 2 * G) // L
    grads = acc[:, :ext_rows].reshape(3, atoms + 2 * G)
    above = lax.ppermute(grads[:, :G], AXES, down)
    below = lax.ppermute(grads[:, atoms + G :], AXES, up)
    raw = -grads[:, G : atoms + G]
    details = (atom_bead.reshape(1, atoms), spread(dest), spread(block_start.astype(F32)))
    last = atoms // CHUNK - 1
    partial = mapping(raw, *details, "mapping_inner", last - 1, lambda i: i + 1)
    above, below, partial = lax.optimization_barrier((above, below, partial))
    force = raw - jnp.pad(below, ((0, 0), (0, atoms - G))) - jnp.pad(above, ((0, 0), (atoms - G, 0)))
    outgoing = mapping(force, *details, "mapping_border", 2, lambda i: i * last, (partial,))
    recv = exchange(outgoing)
    bead_force, sums = bead_stage(
        recv, bead_weight.reshape(1, beads), pred, offs, w_first, second, beads * devices
    )
    grad_one, grad_two, loss = reduce_all(sums)
    return force, bead_force, pred, grad_one, grad_two.reshape(L), loss.reshape(())


def solution(mesh):
    wide = P(None, AXES)
    tall = P(AXES, None)
    flat = P(AXES)
    return jax.shard_map(
        local,
        mesh=mesh,
        in_specs=(
            wide, wide, tall, flat, P(), P(), P(), flat, flat, flat, wide, tall, flat, P(), P(),
        ),
        out_specs=(wide, wide, wide, P(), P(), P()),
        check_vma=False,
    )
```
